512 devices in a mesh: seq: 512 (over y, x, z, core).
Axes of the slice: x: 4, y: 8, z: 8, core: 2. Of those that a mesh axis runs over, the one named last changes fastest.
Arguments:
- queries: bfloat16 [131072, 8, 128], P('seq'), may hold values from -132 to 132
- keys: bfloat16 [262144, 8, 128], P('seq'), may hold values from -6 to 6
- values: bfloat16 [262144, 8, 128], P('seq'), may hold values from -6 to 6
- routes: int32 [131072, 8], P('seq'), may hold values from 0 to 63, all different within a row; in each aligned block of 256 rows (0 to 255, 256 to 511, ...) at most 40 rows name the same one
Outputs:
- attended: bfloat16 [131072, 8, 128], P('seq')
The draws below stay inside these ranges and needn't reach their ends.
Inputs may be any that keep to these rules, and one draw needn't show every extreme that they name: `routes`: each row names 8 different heads; among the 256 rows of one device no head is named more than 40 times, a bound that some block reaches.
All inputs are finite; a program needn't handle non-finite values.
Results may differ from the reference program's by a relative error of at most 0.0065.
Values may be sent and summed in bfloat16 or wider, within the bound.
No kernel may reach another device: no remote copies, remote signals or barrier semaphores. Data moves between devices by JAX's collectives and lax.ppermute only.
A program may use at most 64 MiB of HBM per device.

```python
import math
import jax
import jax.numpy as jnp
import numpy as np
from jax import lax

HEADS = 64
KV_HEADS = 8
HEAD_DIM = 128
ROUTED = 8
HOPS = 4
MOST = 40
QRY_DEV = 256
CTX_DEV = 512
CONTEXT = 262144
QUERIES = 131072


def base_keys(key):
    shards = CONTEXT // CTX_DEV
    normal_keys = jax.random.truncated_normal(jax.random.fold_in(key, 11), -6.0, 6.0, (shards, CTX_DEV, KV_HEADS, HEAD_DIM), jnp.float32)
    return normal_keys


def draw_keys(key, part):
    return base_keys(key).reshape(CONTEXT, KV_HEADS, HEAD_DIM).astype(jnp.bfloat16)


def draw_queries(key, part):
    shards = CONTEXT // CTX_DEV
    drawn = jax.random.truncated_normal(jax.random.fold_in(key, 13), -6.0, 6.0, (shards, QRY_DEV, ROUTED, HEAD_DIM), jnp.float32)
    return drawn.reshape(QUERIES, ROUTED, HEAD_DIM).astype(jnp.bfloat16)


def shard_levels(own_key, extent, cuts, least, high):
    factor_of, own = 1.0, jax.random.fold_in(own_key, 6)
    for axis_at, parts in cuts:
        steps = jnp.exp(jax.random.uniform(jax.random.fold_in(own, axis_at), (parts,), jnp.float32, least / len(cuts), high / len(cuts)))
        factor_of = factor_of * jnp.repeat(steps, extent[axis_at] // parts).reshape([-1 if axis == axis_at else 1 for axis in range(len(extent))])
    return factor_of


def shared_out(rng, own, number, rows, count, top, limit, slope):
    ranking = jax.random.permutation(rng, count)
    crowded, common = load_shares(count, rows * top, limit, slope, True), load_shares(count, rows * top, limit, slope, False)
    places = jnp.arange(count)

    def named(lengths, offset_by):
        used = int((lengths > 0).sum())
        fixed = max(1, used // 4)
        passed = fixed + (places - fixed + offset_by * (used - fixed)) % max(1, count - fixed)
        return jnp.zeros((count,), jnp.int32).at[ranking[jnp.where(places < fixed, places, passed)]].set(jnp.asarray(lengths, jnp.int32))

    lengths = jnp.where(number % 4 == 0, named(crowded, number // 4), named(common, number - number // 4 - 1))
    mixed = jax.random.permutation(jax.random.fold_in(own, 3), count)
    giver, receiver = mixed[0:count // 2 * 2:2], mixed[1:count // 2 * 2:2]
    margin = jnp.minimum(lengths[giver] - 1, limit - lengths[receiver]) // 2
    margin = jnp.where((giver == ranking[0]) | (receiver == ranking[0]) | (lengths[receiver] == 0), 0, jnp.maximum(margin, 0))
    passed = jax.random.randint(jax.random.fold_in(own, 4), (count // 2,), 0, 1 << 20) % (margin + 1)
    lengths = lengths.at[giver].add(-passed).at[receiver].add(passed)
    items = jnp.searchsorted(jnp.cumsum(lengths), jnp.arange(rows * top), side="right").astype(jnp.int32)
    listing = items.reshape(top, rows).T
    listing = listing[jax.random.permutation(jax.random.fold_in(own, 1), rows)]
    offset_by = jax.random.randint(jax.random.fold_in(own, 2), (rows, 1), 0, top)
    return jnp.take_along_axis(listing, (jnp.arange(top)[None, :] + offset_by) % top, axis=1)


def load_shares(count, total, bound, skew, full):
    loads = [(1 << 20) // math.isqrt(grade ** skew) + 1 for grade in range(1, count + 1)]
    largest = bound if full else min(bound, max(-(-total // count), total * loads[0] // sum(loads)))
    least = 1 if total - largest >= count - 1 else 0
    given, spare = [largest] + [least] * (count - 1), total - largest - least * (count - 1)
    while spare > 0:
        free = [i for i in range(1, count) if given[i] < largest] or [i for i in range(1, count) if given[i] < bound]
        mass, left = sum([loads[i] for i in free]), spare
        for i in free:
            addition = min(bound - given[i], max(1, left * loads[i] // mass), spare)
            given[i] = given[i] + addition
            spare = spare - addition
    return np.array(given)


def centred(own_key, shape, width, reach, pieces=(), held_as=jnp.bfloat16):
    loudness = shard_levels(own_key, shape, pieces, -0.22, 0.18) if pieces else 1.0
    values = jax.random.normal(own_key, shape, jnp.float32) * width * loudness
    return jnp.minimum(jnp.maximum(values, -reach), reach).astype(held_as)


def setup_inputs(seed: int = 0) -> dict:
    seeds = jax.random.split(jax.random.key(seed), 5)
    queries = draw_queries(jax.random.fold_in(seeds[4], 71), 0)
    keys = draw_keys(jax.random.fold_in(seeds[4], 71), 0)
    values = centred(seeds[2], (CONTEXT, KV_HEADS, HEAD_DIM), 1.0, 6.0, ((0, 512),))
    routes_keys = jax.random.split(jax.random.fold_in(seeds[3], 1), QUERIES // QRY_DEV)
    routes_turns = jax.random.permutation(jax.random.fold_in(seeds[3], 3), QUERIES // QRY_DEV)
    routes = jax.vmap(lambda own, number: shared_out(jax.random.fold_in(seeds[3], 2), own, number, QRY_DEV, HEADS, ROUTED, MOST, 2))(routes_keys, routes_turns).reshape((QUERIES, ROUTED))
    return {"queries": queries, "keys": keys, "values": values, "routes": routes}


def slot_index(routes_dev):
    flat_heads = routes_dev.reshape(-1)
    heads_all = jnp.arange(HEADS, dtype=jnp.int32)
    onehot = (flat_heads[:, None] == heads_all[None, :]).astype(jnp.int32)
    before = jnp.cumsum(onehot, axis=0) - onehot
    within = lax.optimization_barrier(jnp.sum(before * onehot, axis=1)).astype(jnp.int32)
    return (flat_heads * MOST + within).astype(jnp.int32)

def one_shard(arguments):
    device, query_dev, routes_dev, padded_keys, padded_values = arguments
    slots = slot_index(routes_dev)
    flat = query_dev.reshape(-1, HEAD_DIM)
    packed = jnp.zeros((HEADS * MOST, HEAD_DIM), jnp.float32).at[slots].set(flat.astype(jnp.float32))
    tokens_of = jnp.repeat(jnp.arange(QRY_DEV, dtype=jnp.int32), ROUTED)
    positions = jnp.zeros((HEADS * MOST,), jnp.int32).at[slots].set(tokens_of)
    packed = packed.reshape(KV_HEADS, -1, HEAD_DIM)
    positions = positions.reshape(KV_HEADS, -1)
    window = HOPS + 1
    start = (device * CTX_DEV).astype(jnp.int32)
    win_keys = lax.dynamic_slice_in_dim(padded_keys, start, window * CTX_DEV, 0).astype(jnp.float32)
    win_values = lax.dynamic_slice_in_dim(padded_values, start, window * CTX_DEV, 0).astype(jnp.float32)
    scores = jnp.einsum('gqd,kgd->gqk', packed, win_keys) / jnp.sqrt(jnp.float32(HEAD_DIM))
    column = jnp.arange(window * CTX_DEV, dtype=jnp.int32)
    shard_of = column // CTX_DEV
    inside = device - HOPS + shard_of >= 0
    offset = CTX_DEV - QRY_DEV
    causal = (shard_of < HOPS)[None, None, :] | ((column - HOPS * CTX_DEV)[None, None, :] <= (positions + offset)[:, :, None])
    allowed = inside[None, None, :] & causal
    scores = jnp.where(allowed, scores, jnp.float32(-1e+30))
    highest = lax.optimization_barrier(jnp.max(scores, axis=2))
    weights = jnp.where(allowed, jnp.exp(scores - highest[:, :, None]), jnp.float32(0.0))
    total = lax.optimization_barrier(jnp.sum(weights, axis=2))
    rounded = weights.astype(jnp.bfloat16).astype(jnp.float32)
    output = jnp.einsum('gqk,kgd->gqd', rounded, win_values) / total[:, :, None]
    output = output.astype(jnp.bfloat16).reshape(-1, HEAD_DIM)
    return output[slots].reshape(QRY_DEV, ROUTED, HEAD_DIM)

def reference(queries, keys, values, routes):
    shards = CONTEXT // CTX_DEV
    front = jnp.zeros((HOPS * CTX_DEV, KV_HEADS, HEAD_DIM), keys.dtype)
    padded_keys = jnp.concatenate([front, keys], axis=0)
    padded_values = jnp.concatenate([front, values], axis=0)
    query_all = queries.reshape(shards, QRY_DEV, ROUTED, HEAD_DIM)
    routes_all = routes.reshape(shards, QRY_DEV, ROUTED)
    devices = jnp.arange(shards, dtype=jnp.int32)
    result = lax.map(lambda item: one_shard((item[0], item[1], item[2], padded_keys, padded_values)), (devices, query_all, routes_all))
    return result.reshape(QUERIES, ROUTED, HEAD_DIM)
```

```python
import functools

import jax
import jax.numpy as jnp
from jax import lax
from jax.experimental import pallas as pl
from jax.experimental.pallas import tpu as pltpu
from jax.sharding import PartitionSpec as P

GROUPS = 8
MOST_GROUP = 320
ROWS = 2176
SPAN = ROWS + MOST_GROUP
META = 16
TAIL = 64
BLOCKS = ROWS // 128
CHUNK = 160
STEP = 4
LIMIT = 32 * 2**20
SMALL = pl.CostEstimate(flops=1000, bytes_accessed=1000, transcendentals=0)
LOW = -1e30
SCALE = 1.4426950408889634 / (128.0**0.5)
F32, BF16, I32 = jnp.float32, jnp.bfloat16, jnp.int32


def dot(a, b):
    return jnp.dot(a, b, preferred_element_type=F32)


def dot_t(a, b):
    return lax.dot_general(a, b, (((1,), (1,)), ((), ())), preferred_element_type=F32)


def iota(shape, dim):
    return lax.broadcasted_iota(I32, shape, dim)


def one_hot(mask):
    return jnp.where(mask, F32(1), F32(0)).astype(BF16)


def sort_kernel(routes_ref, q_ref, packed_ref, pos_ref, slots_ref, right):
    routed, tokens = routes_ref.shape
    entries = routed * tokens
    group = lax.shift_right_logical(routes_ref[...], 3)
    hot = jnp.concatenate([jnp.where(group == g, F32(1), F32(0)) for g in range(GROUPS)], axis=0)
    hot16 = hot.astype(BF16)
    before = dot(hot16, one_hot(iota((tokens, tokens), 0) < iota((tokens, tokens), 1)))
    total = dot(hot16, jnp.ones((tokens, tokens), BF16)).astype(BF16)
    side = (GROUPS * routed, GROUPS * routed)
    row, col = iota(side, 0), iota(side, 1)
    same = (row // routed) == (col // routed)
    earlier = dot(one_hot(same & (col < row)), total)
    count = dot(one_hot(same), total).astype(I32)
    sixteens = lax.shift_right_logical(count + 15, 4).astype(F32).astype(BF16)
    first = dot(one_hot(((col // routed) < (row // routed)) & (col % routed == 0)), sixteens)
    places = hot * (before + earlier + 16.0 * first)
    slots = sum(places[g * routed : (g + 1) * routed] for g in range(GROUPS)).astype(I32)
    slots_ref[...] = slots
    line = jnp.concatenate([slots[r : r + 1] for r in range(routed)], axis=1)
    right[:, :128] = q_ref[...]
    right[:, 128:] = (iota((entries, 128), 0) % tokens).astype(F32).astype(BF16)
    for b in range(BLOCKS):
        place = one_hot(iota((128, entries), 0) + b * 128 == line)
        sorted_rows = dot(place, right[...])
        packed_ref[b * 128 : (b + 1) * 128] = sorted_rows[:, :128].astype(BF16)
        pos_ref[b * 128 : (b + 1) * 128] = sorted_rows[:, 128:].astype(BF16)
    starts = jnp.concatenate([first[g * routed : g * routed + 1, :128] for g in range(GROUPS)], axis=0)
    packed_ref[ROWS : ROWS + META] = jnp.concatenate([starts, jnp.zeros_like(starts)], axis=0).astype(BF16)


def sort_queries(routes_t, queries_r):
    routed, tokens = routes_t.shape
    return pl.pallas_call(
        sort_kernel,
        out_shape=[
            jax.ShapeDtypeStruct((ROWS + META, 128), BF16),
            jax.ShapeDtypeStruct((ROWS, 128), BF16),
            jax.ShapeDtypeStruct((routed, tokens), I32),
        ],
        scratch_shapes=[pltpu.VMEM((routed * tokens, 256), BF16)],
        compiler_params=pltpu.CompilerParams(vmem_limit_bytes=24 * 2**20),
        cost_estimate=SMALL,
        name="sort_queries",
    )(routes_t, queries_r)


def attend_kernel(kind, info, q_ref, *refs):
    kv_count = {"own": 2, "near": 3, "far": 2}[kind]
    kv = refs[:kv_count]
    refs = refs[kv_count:]
    if kind == "own":
        pos_ref, out_ref, lse_ref, qs, os, ls, ps = refs
    else:
        out_ref, qs, os, ls, tail = refs
    step = pl.program_id(0)
    odd, chip = info[8], info[9]

    def shard_parts(i, most):
        first = [(kv[0][0, i], kv[0][1, i], None, False)]
        second = [(kv[1][0, i], kv[1][1, i], None, False)]
        if kind == "own":
            first = [
                (kv[0][0, i, :256], kv[0][1, i, :256], None, False),
                (kv[0][0, i, 256:], kv[0][1, i, 256:], None, True),
            ]
        if kind == "near" and most == 3:
            flag = jnp.where(chip >= 1, F32(0), F32(LOW))
            second.append((kv[2][0, i], kv[2][1, i], flag, False))
        return first if most == 1 else first + second

    def work(most):
        @pl.when(step == 0)
        def _():
            qs[:ROWS] = q_ref[:ROWS]
            os[...] = jnp.zeros_like(os)
            ls[...] = jnp.zeros_like(ls)
            if kind == "own":
                ps[:ROWS] = pos_ref[...]

        units = []
        for i in range(STEP):
            start = pl.multiple_of(info[step * STEP + i] * 16, 16)
            parts = shard_parts(i, most)
            for c in range(MOST_GROUP // CHUNK):
                units.append((pl.ds(pl.multiple_of(start + c * CHUNK, 16), CHUNK), parts))
        scored = []
        for rows, parts in units:
            q = qs[rows, :]
            scores = []
            for k, _, _, causal in parts:
                s = dot_t(q, k)
                if causal:
                    reach = ps[rows, :].astype(F32)[:, :1]
                    s = jnp.where(iota(s.shape, 1).astype(F32) <= reach, s, F32(LOW))
                scores.append(s)
            scored.append(scores)
        tops = []
        for (rows, parts), scores in zip(units, scored):
            peaks = []
            for s, (_, _, bias, _) in zip(scores, parts):
                peak = jnp.max(s, axis=1, keepdims=True)
                peaks.append(peak if bias is None else peak + bias)
            tops.append(functools.reduce(jnp.maximum, peaks))
        results = []
        for (rows, parts), scores, top in zip(units, scored, tops):
            both = None
            for s, (_, v, bias, _) in zip(scores, parts):
                base = top if bias is None else top - bias
                weight = jnp.exp2((s - base) * F32(SCALE)).astype(BF16)
                product = dot(weight, jnp.concatenate([v, jnp.ones_like(v)], axis=1))
                both = product if both is None else both + product
            results.append(both)
        for (rows, parts), both, top in zip(units, results, tops):
            total = both[:, 128:]
            os[rows, :] = (both[:, :128] / total).astype(BF16)
            ls[rows, :] = top * F32(SCALE) + jnp.log2(total)

        @pl.when(step == GROUPS // STEP - 1)
        def _():
            out_ref[:ROWS] = os[:ROWS]
            if kind == "own":
                lse_ref[...] = ls[:ROWS]
            else:
                eye = iota((128, 128), 0) == iota((128, 128), 1)
                tail[...] = jnp.zeros_like(tail)
                for b in range(BLOCKS):
                    square = ls[b * 128 : (b + 1) * 128]
                    line = jnp.sum(jnp.where(eye, square, F32(0)), axis=0, keepdims=True)
                    high = line.astype(BF16).astype(F32)
                    middle = (line - high).astype(BF16).astype(F32)
                    tail[b : b + 1] = high
                    tail[BLOCKS + b : BLOCKS + b + 1] = middle
                    tail[2 * BLOCKS + b : 2 * BLOCKS + b + 1] = line - high - middle
                out_ref[ROWS:] = tail[...].astype(BF16)

    even_most, odd_most = {"own": (1, 2), "near": (2, 3), "far": (2, 0)}[kind]
    pl.when(odd == 0)(lambda: work(even_most))
    if odd_most:
        pl.when(odd == 1)(lambda: work(odd_most))


def attend(kind, info, packed, kvs, pos=None):
    kv_spec = pl.BlockSpec((2, STEP, 512, 128), lambda g: (0, g, 0, 0))

    def whole(rows):
        return pl.BlockSpec((rows, 128), lambda g: (0, 0))

    in_specs = [pl.BlockSpec(memory_space=pltpu.SMEM), whole(ROWS + META)] + [kv_spec] * len(kvs)
    args = [info, packed, *kvs]
    scratch = [pltpu.VMEM((SPAN, 128), BF16), pltpu.VMEM((SPAN, 128), BF16), pltpu.VMEM((SPAN, 128), F32)]
    if kind == "own":
        in_specs.append(whole(ROWS))
        args.append(pos)
        out_shape = [jax.ShapeDtypeStruct((ROWS, 128), BF16), jax.ShapeDtypeStruct((ROWS, 128), F32)]
        out_specs = [whole(ROWS), whole(ROWS)]
        scratch.append(pltpu.VMEM((SPAN, 128), BF16))
    else:
        out_shape = jax.ShapeDtypeStruct((ROWS + TAIL, 128), BF16)
        out_specs = whole(ROWS + TAIL)
        scratch.append(pltpu.VMEM((TAIL, 128), F32))
    return pl.pallas_call(
        functools.partial(attend_kernel, kind),
        grid=(GROUPS // STEP,),
        in_specs=in_specs,
        out_specs=out_specs,
        out_shape=out_shape,
        scratch_shapes=scratch,
        compiler_params=pltpu.CompilerParams(
            dimension_semantics=("arbitrary",), vmem_limit_bytes=LIMIT
        ),
        cost_estimate=SMALL,
        name="attend_" + kind,
    )(*args)


def finish_kernel(info, own_ref, lse_ref, near_ref, far_ref, slots_ref, out_ref, merged):
    odd, chip = info[8], info[9]
    near_on = chip >= 1
    far_on = (chip >= 2) & (odd == 0)
    eye = iota((128, 128), 0) == iota((128, 128), 1)

    def lines(ref):
        tail = ref[ROWS:].astype(F32)
        return tail[:BLOCKS] + tail[BLOCKS : 2 * BLOCKS] + tail[2 * BLOCKS : 3 * BLOCKS]

    near_lines, far_lines = lines(near_ref), lines(far_ref)
    for b in range(BLOCKS):
        rows = slice(b * 128, (b + 1) * 128)
        own = lse_ref[rows]

        def column(table, on):
            picked = jnp.where(eye, table[b : b + 1], F32(0))
            return jnp.where(on, jnp.sum(picked, axis=1, keepdims=True), F32(LOW))

        near, far = column(near_lines, near_on), column(far_lines, far_on)
        top = jnp.maximum(own, jnp.maximum(near, far))
        a, n, f = jnp.exp2(own - top), jnp.exp2(near - top), jnp.exp2(far - top)
        mixed = a * own_ref[rows].astype(F32) + n * near_ref[rows].astype(F32) + f * far_ref[rows].astype(F32)
        merged[rows] = (mixed / (a + n + f)).astype(BF16)
    entries = out_ref.shape[0]
    for e in range(entries // 256):
        rows = slice(e * 256, (e + 1) * 256)
        place = one_hot(iota((256, ROWS), 1) == slots_ref[rows])
        out_ref[rows] = dot(place, merged[...]).astype(BF16)


def finish(info, own, lse, near, far, slots_column):
    entries = slots_column.shape[0]
    return pl.pallas_call(
        finish_kernel,
        in_specs=[pl.BlockSpec(memory_space=pltpu.SMEM)] + [pl.BlockSpec(memory_space=pltpu.VMEM)] * 5,
        out_shape=jax.ShapeDtypeStruct((entries, 128), BF16),
        scratch_shapes=[pltpu.VMEM((ROWS, 128), BF16)],
        compiler_params=pltpu.CompilerParams(vmem_limit_bytes=24 * 2**20),
        cost_estimate=SMALL,
        name="finish",
    )(info, own, lse, near, far, slots_column)


def moved(block, distance, sources=lambda i: True):
    devices = range(lax.axis_size("seq"))
    return lax.ppermute(
        block, "seq", [(i, i + distance) for i in devices if sources(i) and i + distance in devices]
    )


def odd_device(i):
    return i % 2 == 1


def even_device(i):
    return i % 2 == 0


def shards(queries, keys, values, routes):
    tokens, routed, width = queries.shape
    devices = range(lax.axis_size("seq"))
    device = lax.axis_index("seq").astype(I32)
    flags = jnp.stack([device % 2, device // 2])

    def info(packed):
        return jnp.concatenate([packed[ROWS : ROWS + 8, 0].astype(I32), flags])

    def after(x, *others):
        return lax.optimization_barrier((x, *others))[0]

    kv = jnp.stack([keys.transpose(1, 0, 2), values.transpose(1, 0, 2)])
    kv_forward = moved(kv, 2, odd_device)
    packed, pos, slots = sort_queries(after(routes.T, kv), queries.transpose(1, 0, 2).reshape(-1, width))
    column = slots.T.reshape(-1, 1)
    own_info = info(packed)
    far_q = moved(packed, -4, even_device)
    kv_sibling = lax.ppermute(after(kv, packed), "seq", [(i, i ^ 1) for i in devices])
    own, lse = attend("own", own_info, packed, [kv, kv_sibling], pos)
    near_q = moved(after(packed, own, column), -2)
    far_q = after(far_q, own)
    far_out = attend("far", info(far_q), far_q, [kv, kv_sibling])
    far_back = moved(far_out, 4, even_device)
    near_q = after(near_q, far_out)
    near_back = moved(attend("near", info(near_q), near_q, [kv, kv_sibling, kv_forward]), 2)
    out = finish(own_info, own, lse, near_back, far_back, column)
    return out.reshape(tokens, routed, width)


def solution(mesh):
    placed = (P("seq", None, None), P("seq", None, None), P("seq", None, None), P("seq", None))
    return jax.shard_map(
        shards, mesh=mesh, in_specs=placed, out_specs=P("seq", None, None), check_vma=False
    )
```

```python
import functools

import jax
import jax.numpy as jnp
from jax import lax
from jax.experimental import pallas as pl
from jax.experimental.pallas import tpu as pltpu
from jax.sharding import PartitionSpec as P

GROUPS = 8
MOST_GROUP = 320
ROWS = 2176
SPAN = ROWS + MOST_GROUP
META = 16
TAIL = 64
BLOCKS = ROWS // 128
LINES = 24
CHUNK = 160
STEP = 4
LIMIT = 32 * 2**20
SMALL = pl.CostEstimate(flops=1000, bytes_accessed=1000, transcendentals=0)
LOW = -1e30
SCALE = 1.4426950408889634 / (128.0**0.5)
F32, BF16, I32 = jnp.float32, jnp.bfloat16, jnp.int32


def dot(a, b):
    return jnp.dot(a, b, preferred_element_type=F32)


def dot_t(a, b):
    return lax.dot_general(a, b, (((1,), (1,)), ((), ())), preferred_element_type=F32)


def iota(shape, dim):
    return lax.broadcasted_iota(I32, shape, dim)


def one_hot(mask):
    return jnp.where(mask, F32(1), F32(0)).astype(BF16)


def sort_kernel(routes_ref, q_ref, packed_ref, pos_ref, slots_ref, right):
    routed, tokens = routes_ref.shape
    entries = routed * tokens
    group = lax.shift_right_logical(routes_ref[...], 3)
    hot = jnp.concatenate([jnp.where(group == g, F32(1), F32(0)) for g in range(GROUPS)], axis=0)
    hot16 = hot.astype(BF16)
    before = dot(hot16, one_hot(iota((tokens, tokens), 0) < iota((tokens, tokens), 1)))
    total = dot(hot16, jnp.ones((tokens, tokens), BF16)).astype(BF16)
    side = (GROUPS * routed, GROUPS * routed)
    row, col = iota(side, 0), iota(side, 1)
    same = (row // routed) == (col // routed)
    earlier = dot(one_hot(same & (col < row)), total)
    count = dot(one_hot(same), total).astype(I32)
    sixteens = lax.shift_right_logical(count + 15, 4).astype(F32).astype(BF16)
    first = dot(one_hot(((col // routed) < (row // routed)) & (col % routed == 0)), sixteens)
    places = hot * (before + earlier + 16.0 * first)
    slots = sum(places[g * routed : (g + 1) * routed] for g in range(GROUPS)).astype(I32)
    slots_ref[...] = slots
    line = jnp.concatenate([slots[r : r + 1] for r in range(routed)], axis=1)
    right[:, :128] = q_ref[...]
    right[:, 128:] = (iota((entries, 128), 0) % tokens).astype(F32).astype(BF16)
    eye = iota((128, 128), 0) == iota((128, 128), 1)
    pos_ref[...] = jnp.zeros_like(pos_ref)
    for b in range(BLOCKS):
        place = one_hot(iota((128, entries), 0) + b * 128 == line)
        sorted_rows = dot(place, right[...])
        packed_ref[b * 128 : (b + 1) * 128] = sorted_rows[:, :128].astype(BF16)
        pos_ref[b : b + 1] = jnp.sum(jnp.where(eye, sorted_rows[:, 128:], F32(0)), axis=0, keepdims=True)
    starts = jnp.concatenate([first[g * routed : g * routed + 1, :128] for g in range(GROUPS)], axis=0)
    packed_ref[ROWS : ROWS + META] = jnp.concatenate([starts, jnp.zeros_like(starts)], axis=0).astype(BF16)


def sort_queries(routes_t, queries_r):
    routed, tokens = routes_t.shape
    return pl.pallas_call(
        sort_kernel,
        out_shape=[
            jax.ShapeDtypeStruct((ROWS + META, 128), BF16),
            jax.ShapeDtypeStruct((LINES, 128), F32),
            jax.ShapeDtypeStruct((routed, tokens), I32),
        ],
        scratch_shapes=[pltpu.VMEM((routed * tokens, 256), BF16)],
        compiler_params=pltpu.CompilerParams(vmem_limit_bytes=24 * 2**20),
        cost_estimate=SMALL,
        name="sort_queries",
    )(routes_t, queries_r)


def attend_kernel(kind, flags, *refs):
    q_count, kv_count = {"own": (1, 1), "near": (1, 3), "far": (2, 2)}[kind]
    q_refs, refs = refs[:q_count], refs[q_count:]
    kv, refs = refs[:kv_count], refs[kv_count:]
    if kind == "own":
        pos_ref, out_ref, qs, os, ls, tail, starts, ps = refs
    else:
        out_ref, qs, os, ls, tail, starts = refs
    step = pl.program_id(0)
    odd, chip = flags[0], flags[1]

    def shard_parts(i, is_odd):
        if kind == "own":
            return [
                (kv[0][0, i, :256], kv[0][1, i, :256], None, False),
                (kv[0][0, i, 256:], kv[0][1, i, 256:], None, True),
            ]
        sibling = (kv[1][0, i], kv[1][1, i], None, False)
        if kind == "far" and is_odd:
            return [sibling]
        parts = [(kv[0][0, i], kv[0][1, i], None, False), sibling]
        if is_odd:
            flag = jnp.where(chip >= 1, F32(0), F32(LOW))
            parts.append((kv[2][0, i], kv[2][1, i], flag, False))
        return parts

    def work(is_odd):
        @pl.when(step == 0)
        def _():
            if kind == "far" and is_odd:
                pltpu.sync_copy(q_refs[1], qs.at[pl.ds(0, ROWS + META)])
            else:
                qs[: ROWS + META] = q_refs[0][...]
            os[...] = jnp.zeros_like(os)
            ls[...] = jnp.zeros_like(ls)
            firsts = qs[ROWS : ROWS + META].astype(F32)
            for g in range(GROUPS):
                starts[g] = jnp.max(firsts[g : g + 1]).astype(I32)
            if kind == "own":
                eye = iota((128, 128), 0) == iota((128, 128), 1)
                for b in range(BLOCKS):
                    picked = jnp.where(eye, pos_ref[b : b + 1], F32(0))
                    reach = jnp.sum(picked, axis=1, keepdims=True)
                    ps[b * 128 : (b + 1) * 128] = jnp.broadcast_to(reach, (128, 128))

        units = []
        for i in range(STEP):
            start = pl.multiple_of(starts[step * STEP + i] * 16, 16)
            parts = shard_parts(i, is_odd)
            for c in range(MOST_GROUP // CHUNK):
                units.append((pl.ds(pl.multiple_of(start + c * CHUNK, 16), CHUNK), parts))
        scored = []
        for rows, parts in units:
            q = qs[rows, :]
            scores = []
            for k, _, _, causal in parts:
                s = dot_t(q, k)
                if causal:
                    reach = ps[rows, :][:, :1]
                    s = jnp.where(iota(s.shape, 1).astype(F32) <= reach, s, F32(LOW))
                scores.append(s)
            scored.append(scores)
        tops = []
        for (rows, parts), scores in zip(units, scored):
            peaks = []
            for s, (_, _, bias, _) in zip(scores, parts):
                peak = jnp.max(s, axis=1, keepdims=True)
                peaks.append(peak if bias is None else peak + bias)
            tops.append(functools.reduce(jnp.maximum, peaks))
        results = []
        for (rows, parts), scores, top in zip(units, scored, tops):
            both = None
            for s, (_, v, bias, _) in zip(scores, parts):
                base = top if bias is None else top - bias
                weight = jnp.exp2((s - base) * F32(SCALE)).astype(BF16)
                product = dot(weight, jnp.concatenate([v, jnp.ones_like(v)], axis=1))
                both = product if both is None else both + product
            results.append(both)
        for (rows, parts), both, top in zip(units, results, tops):
            total = both[:, 128:]
            os[rows, :] = (both[:, :128] / total).astype(BF16)
            ls[rows, :] = top * F32(SCALE) + jnp.log2(total)

        @pl.when(step == GROUPS // STEP - 1)
        def _():
            out_ref[:ROWS] = os[:ROWS]
            eye = iota((128, 128), 0) == iota((128, 128), 1)
            tail[...] = jnp.zeros_like(tail)
            for b in range(BLOCKS):
                square = ls[b * 128 : (b + 1) * 128]
                line = jnp.sum(jnp.where(eye, square, F32(0)), axis=0, keepdims=True)
                high = line.astype(BF16).astype(F32)
                middle = (line - high).astype(BF16).astype(F32)
                tail[b : b + 1] = high
                tail[BLOCKS + b : BLOCKS + b + 1] = middle
                tail[2 * BLOCKS + b : 2 * BLOCKS + b + 1] = line - high - middle
            out_ref[ROWS:] = tail[...].astype(BF16)

    if kind == "own":
        work(False)
    else:
        pl.when(odd == 0)(lambda: work(False))
        pl.when(odd == 1)(lambda: work(True))


def attend(kind, flags, packed, kvs, pos=None):
    kv_spec = pl.BlockSpec((2, STEP, 512, 128), lambda g: (0, g, 0, 0))

    def whole(rows):
        return pl.BlockSpec((rows, 128), lambda g: (0, 0))

    in_specs = [pl.BlockSpec(memory_space=pltpu.SMEM)]
    in_specs += [whole(ROWS + META)] + [pl.BlockSpec(memory_space=pltpu.HBM)] * (len(packed) - 1)
    in_specs += [kv_spec] * len(kvs)
    args = [flags, *packed, *kvs]
    scratch = [pltpu.VMEM((SPAN, 128), BF16), pltpu.VMEM((SPAN, 128), BF16), pltpu.VMEM((SPAN, 128), F32)]
    scratch += [pltpu.VMEM((TAIL, 128), F32), pltpu.SMEM((GROUPS,), I32)]
    if kind == "own":
        in_specs.append(whole(LINES))
        args.append(pos)
        scratch.append(pltpu.VMEM((SPAN, 128), F32))
    return pl.pallas_call(
        functools.partial(attend_kernel, kind),
        grid=(GROUPS // STEP,),
        in_specs=in_specs,
        out_specs=whole(ROWS + TAIL),
        out_shape=jax.ShapeDtypeStruct((ROWS + TAIL, 128), BF16),
        scratch_shapes=scratch,
        compiler_params=pltpu.CompilerParams(
            dimension_semantics=("arbitrary",), vmem_limit_bytes=LIMIT
        ),
        cost_estimate=SMALL,
        name="attend_" + kind,
    )(*args)


def lines_of(tail):
    tail = tail.astype(F32)
    return tail[:BLOCKS] + tail[BLOCKS : 2 * BLOCKS] + tail[2 * BLOCKS : 3 * BLOCKS]


def mix(lines, b, on):
    first, second = lines[0][b : b + 1], jnp.where(on, lines[1][b : b + 1], F32(LOW))
    top = jnp.maximum(first, second)
    total = jnp.exp2(first - top) + jnp.exp2(second - top)
    eye = iota((128, 128), 0) == iota((128, 128), 1)
    share = jnp.exp2(second - top) / total
    column = jnp.sum(jnp.where(eye, share, F32(0)), axis=1, keepdims=True)
    return column, top + jnp.log2(total)


def mix_kernel(flags, own_ref, back_ref, here_ref, sum_ref, lines_ref):
    odd, chip = flags[0], flags[1]

    def run(other, on):
        lines = lines_of(own_ref[ROWS:]), lines_of(other[ROWS:])
        lines_ref[...] = jnp.zeros_like(lines_ref)
        for b in range(BLOCKS):
            rows = slice(b * 128, (b + 1) * 128)
            share, line = mix(lines, b, on)
            own = own_ref[rows].astype(F32)
            sum_ref[rows] = (own + share * (other[rows].astype(F32) - own)).astype(BF16)
            lines_ref[b : b + 1] = line

    pl.when(odd == 0)(lambda: run(back_ref, chip >= 1))
    pl.when(odd == 1)(lambda: run(here_ref, odd == 1))


def mix_early(flags, own, back, here):
    return pl.pallas_call(
        mix_kernel,
        in_specs=[pl.BlockSpec(memory_space=pltpu.SMEM)] + [pl.BlockSpec(memory_space=pltpu.VMEM)] * 3,
        out_shape=[jax.ShapeDtypeStruct((ROWS, 128), BF16), jax.ShapeDtypeStruct((LINES, 128), F32)],
        compiler_params=pltpu.CompilerParams(vmem_limit_bytes=24 * 2**20),
        cost_estimate=SMALL,
        name="mix_early",
    )(flags, own, back, here)


def finish_kernel(flags, sum_ref, lines_ref, near_ref, far_ref, slots_ref, out_ref, merged):
    odd, chip = flags[0], flags[1]

    def merge(late_ref, on):
        lines = lines_ref[:BLOCKS], lines_of(late_ref[ROWS:])
        for b in range(BLOCKS):
            rows = slice(b * 128, (b + 1) * 128)
            share, _ = mix(lines, b, on)
            early = sum_ref[rows].astype(F32)
            merged[rows] = (early + share * (late_ref[rows].astype(F32) - early)).astype(BF16)

    pl.when(odd == 1)(lambda: merge(near_ref, chip >= 1))
    pl.when(odd == 0)(lambda: merge(far_ref, chip >= 2))
    entries = out_ref.shape[0]
    for e in range(entries // 256):
        rows = slice(e * 256, (e + 1) * 256)
        place = one_hot(iota((256, ROWS), 1) == slots_ref[rows])
        out_ref[rows] = dot(place, merged[...]).astype(BF16)


def finish(flags, early, lines, near, far, slots_column):
    entries = slots_column.shape[0]
    return pl.pallas_call(
        finish_kernel,
        in_specs=[pl.BlockSpec(memory_space=pltpu.SMEM)] + [pl.BlockSpec(memory_space=pltpu.VMEM)] * 5,
        out_shape=jax.ShapeDtypeStruct((entries, 128), BF16),
        scratch_shapes=[pltpu.VMEM((ROWS, 128), BF16)],
        compiler_params=pltpu.CompilerParams(vmem_limit_bytes=24 * 2**20),
        cost_estimate=SMALL,
        name="finish",
    )(flags, early, lines, near, far, slots_column)


def moved(block, distance):
    devices = range(lax.axis_size("seq"))
    pairs = [(i, i + distance(i)) for i in devices if distance(i) and i + distance(i) in devices]
    return lax.ppermute(block, "seq", pairs)


def shards(queries, keys, values, routes):
    tokens, routed, width = queries.shape
    devices = range(lax.axis_size("seq"))
    device = lax.axis_index("seq").astype(I32)
    flags = jnp.stack([device % 2, device // 2])

    def after(x, *others):
        return lax.optimization_barrier((x, *others))[0]

    kv = jnp.stack([keys.transpose(1, 0, 2), values.transpose(1, 0, 2)])
    kv_forward = moved(kv, lambda i: 2 if i % 2 else 0)
    packed, pos, slots = sort_queries(after(routes.T, kv), queries.transpose(1, 0, 2).reshape(-1, width))
    column = slots.T.reshape(-1, 1)
    near_q = moved(packed, lambda i: -2)
    own = attend("own", flags, [packed], [kv], pos)
    kv_sibling = moved(kv, lambda i: -1 if i % 2 else 1)
    far_q = moved(after(packed, own, column), lambda i: 0 if i % 2 else -4)
    near_q = after(near_q, own)
    near_out = attend("near", flags, [near_q], [kv, kv_sibling, kv_forward])
    near_back = moved(near_out, lambda i: 2)
    far_q = after(far_q, near_out)
    far_out = attend("far", flags, [far_q, packed], [kv, kv_sibling])
    far_back = moved(far_out, lambda i: 0 if i % 2 else 4)
    early_sum, early_lines = mix_early(flags, own, near_back, far_out)
    out = finish(flags, early_sum, early_lines, near_back, after(far_back, early_sum), column)
    return out.reshape(tokens, routed, width)


def solution(mesh):
    placed = (P("seq", None, None), P("seq", None, None), P("seq", None, None), P("seq", None))
    return jax.shard_map(
        shards, mesh=mesh, in_specs=placed, out_specs=P("seq", None, None), check_vma=False
    )
```

```python
import functools

import jax
import jax.numpy as jnp
from jax import lax
from jax.experimental import pallas as pl
from jax.experimental.pallas import tpu as pltpu
from jax.sharding import PartitionSpec as P

GROUPS = 8
MOST_GROUP = 320
ROWS = 2176
SPAN = ROWS + MOST_GROUP
META = 16
TAIL = 64
BLOCKS = ROWS // 128
LINES = 24
CHUNK = 160
STEP = 4
LIMIT = 32 * 2**20
SMALL = pl.CostEstimate(flops=1000, bytes_accessed=1000, transcendentals=0)
LOW = -1e30
SCALE = 1.4426950408889634 / (128.0**0.5)
F32, BF16, I32 = jnp.float32, jnp.bfloat16, jnp.int32


def dot(a, b):
    return jnp.dot(a, b, preferred_element_type=F32)


def dot_t(a, b):
    return lax.dot_general(a, b, (((1,), (1,)), ((), ())), preferred_element_type=F32)


def iota(shape, dim):
    return lax.broadcasted_iota(I32, shape, dim)


def one_hot(mask):
    return jnp.where(mask, F32(1), F32(0)).astype(BF16)


def sort_kernel(routes_ref, q_ref, packed_ref, pos_ref, slots_ref, right):
    routed, tokens = routes_ref.shape
    entries = routed * tokens
    group = lax.shift_right_logical(routes_ref[...], 3)
    hot = jnp.concatenate([jnp.where(group == g, F32(1), F32(0)) for g in range(GROUPS)], axis=0)
    hot16 = hot.astype(BF16)
    before = dot(hot16, one_hot(iota((tokens, tokens), 0) < iota((tokens, tokens), 1)))
    total = dot(hot16, jnp.ones((tokens, tokens), BF16)).astype(BF16)
    side = (GROUPS * routed, GROUPS * routed)
    row, col = iota(side, 0), iota(side, 1)
    same = (row // routed) == (col // routed)
    earlier = dot(one_hot(same & (col < row)), total)
    count = dot(one_hot(same), total).astype(I32)
    sixteens = lax.shift_right_logical(count + 15, 4).astype(F32).astype(BF16)
    first = dot(one_hot(((col // routed) < (row // routed)) & (col % routed == 0)), sixteens)
    places = hot * (before + earlier + 16.0 * first)
    slots = sum(places[g * routed : (g + 1) * routed] for g in range(GROUPS)).astype(I32)
    slots_ref[...] = slots
    line = jnp.concatenate([slots[r : r + 1] for r in range(routed)], axis=1)
    right[:, :128] = q_ref[...]
    right[:, 128:] = (iota((entries, 128), 0) % tokens).astype(F32).astype(BF16)
    eye = iota((128, 128), 0) == iota((128, 128), 1)
    pos_ref[...] = jnp.zeros_like(pos_ref)
    for b in range(BLOCKS):
        place = one_hot(iota((128, entries), 0) + b * 128 == line)
        sorted_rows = dot(place, right[...])
        packed_ref[b * 128 : (b + 1) * 128] = sorted_rows[:, :128].astype(BF16)
        pos_ref[b : b + 1] = jnp.sum(jnp.where(eye, sorted_rows[:, 128:], F32(0)), axis=0, keepdims=True)
    starts = jnp.concatenate([first[g * routed : g * routed + 1, :128] for g in range(GROUPS)], axis=0)
    packed_ref[ROWS : ROWS + META] = jnp.concatenate([starts, jnp.zeros_like(starts)], axis=0).astype(BF16)


def sort_queries(routes_t, queries_r):
    routed, tokens = routes_t.shape
    return pl.pallas_call(
        sort_kernel,
        out_shape=[
            jax.ShapeDtypeStruct((ROWS + META, 128), BF16),
            jax.ShapeDtypeStruct((LINES, 128), F32),
            jax.ShapeDtypeStruct((routed, tokens), I32),
        ],
        scratch_shapes=[pltpu.VMEM((routed * tokens, 256), BF16)],
        compiler_params=pltpu.CompilerParams(vmem_limit_bytes=24 * 2**20),
        cost_estimate=SMALL,
        name="sort_queries",
    )(routes_t, queries_r)


def attend_kernel(kind, flags, *refs):
    q_count, kv_count = {"own": (1, 1), "near": (1, 3), "far": (2, 2)}[kind]
    q_refs, refs = refs[:q_count], refs[q_count:]
    kv, refs = refs[:kv_count], refs[kv_count:]
    if kind == "own":
        pos_ref, out_ref, qs, os, ls, tail, starts, ps = refs
    else:
        out_ref, qs, os, ls, tail, starts = refs
    step = pl.program_id(0)
    odd, chip = flags[0], flags[1]

    def shard_parts(i, is_odd):
        if kind == "own":
            return [
                (kv[0][0, i, :256], kv[0][1, i, :256], None, False),
                (kv[0][0, i, 256:], kv[0][1, i, 256:], None, True),
            ]
        parts = [(kv[0][0, i], kv[0][1, i], None, False)]
        if kind == "far" and is_odd:
            return parts
        parts.append((kv[1][0, i], kv[1][1, i], None, False))
        if is_odd:
            flag = jnp.where(chip >= 1, F32(0), F32(LOW))
            parts.append((kv[2][0, i], kv[2][1, i], flag, False))
        return parts

    def work(is_odd):
        @pl.when(step == 0)
        def _():
            if kind == "far" and is_odd:
                pltpu.sync_copy(q_refs[1], qs.at[pl.ds(0, ROWS + META)])
            else:
                qs[: ROWS + META] = q_refs[0][...]
            os[...] = jnp.zeros_like(os)
            ls[...] = jnp.zeros_like(ls)
            firsts = qs[ROWS : ROWS + META].astype(F32)
            for g in range(GROUPS):
                starts[g] = jnp.max(firsts[g : g + 1]).astype(I32)
            if kind == "own":
                eye = iota((128, 128), 0) == iota((128, 128), 1)
                for b in range(BLOCKS):
                    picked = jnp.where(eye, pos_ref[b : b + 1], F32(0))
                    reach = jnp.sum(picked, axis=1, keepdims=True)
                    ps[b * 128 : (b + 1) * 128] = jnp.broadcast_to(reach, (128, 128))

        units = []
        for i in range(STEP):
            start = pl.multiple_of(starts[step * STEP + i] * 16, 16)
            parts = shard_parts(i, is_odd)
            for c in range(MOST_GROUP // CHUNK):
                units.append((pl.ds(pl.multiple_of(start + c * CHUNK, 16), CHUNK), parts))
        scored = []
        for rows, parts in units:
            q = qs[rows, :]
            scores = []
            for k, _, _, causal in parts:
                s = dot_t(q, k)
                if causal:
                    reach = ps[rows, :][:, :1]
                    s = jnp.where(iota(s.shape, 1).astype(F32) <= reach, s, F32(LOW))
                scores.append(s)
            scored.append(scores)
        tops = []
        for (rows, parts), scores in zip(units, scored):
            peaks = []
            for s, (_, _, bias, _) in zip(scores, parts):
                peak = jnp.max(s, axis=1, keepdims=True)
                peaks.append(peak if bias is None else peak + bias)
            tops.append(functools.reduce(jnp.maximum, peaks))
        results = []
        for (rows, parts), scores, top in zip(units, scored, tops):
            both = None
            for s, (_, v, bias, _) in zip(scores, parts):
                base = top if bias is None else top - bias
                weight = jnp.exp2((s - base) * F32(SCALE)).astype(BF16)
                product = dot(weight, jnp.concatenate([v, jnp.ones_like(v)], axis=1))
                both = product if both is None else both + product
            results.append(both)
        for (rows, parts), both, top in zip(units, results, tops):
            total = both[:, 128:]
            os[rows, :] = (both[:, :128] / total).astype(BF16)
            ls[rows, :] = top * F32(SCALE) + jnp.log2(total)

        @pl.when(step == GROUPS // STEP - 1)
        def _():
            out_ref[:ROWS] = os[:ROWS]
            eye = iota((128, 128), 0) == iota((128, 128), 1)
            tail[...] = jnp.zeros_like(tail)
            for b in range(BLOCKS):
                square = ls[b * 128 : (b + 1) * 128]
                line = jnp.sum(jnp.where(eye, square, F32(0)), axis=0, keepdims=True)
                high = line.astype(BF16).astype(F32)
                middle = (line - high).astype(BF16).astype(F32)
                tail[b : b + 1] = high
                tail[BLOCKS + b : BLOCKS + b + 1] = middle
                tail[2 * BLOCKS + b : 2 * BLOCKS + b + 1] = line - high - middle
            out_ref[ROWS:] = tail[...].astype(BF16)

    if kind == "own":
        work(False)
    else:
        pl.when(odd == 0)(lambda: work(False))
        pl.when(odd == 1)(lambda: work(True))


def attend(kind, flags, packed, kvs, pos=None):
    kv_spec = pl.BlockSpec((2, STEP, 512, 128), lambda g: (0, g, 0, 0))
    first = pl.BlockSpec((None, 2, STEP, 512, 128), lambda g: (0, 0, g, 0, 0))
    second = pl.BlockSpec((None, 2, STEP, 512, 128), lambda g: (1, 0, g, 0, 0))
    kv_specs = {"own": [kv_spec], "near": [first, second, kv_spec], "far": [first, second]}[kind]

    def whole(rows):
        return pl.BlockSpec((rows, 128), lambda g: (0, 0))

    in_specs = [pl.BlockSpec(memory_space=pltpu.SMEM)]
    in_specs += [whole(ROWS + META)] + [pl.BlockSpec(memory_space=pltpu.HBM)] * (len(packed) - 1)
    in_specs += kv_specs
    args = [flags, *packed, *kvs]
    scratch = [pltpu.VMEM((SPAN, 128), BF16), pltpu.VMEM((SPAN, 128), BF16), pltpu.VMEM((SPAN, 128), F32)]
    scratch += [pltpu.VMEM((TAIL, 128), F32), pltpu.SMEM((GROUPS,), I32)]
    if kind == "own":
        in_specs.append(whole(LINES))
        args.append(pos)
        scratch.append(pltpu.VMEM((SPAN, 128), F32))
    return pl.pallas_call(
        functools.partial(attend_kernel, kind),
        grid=(GROUPS // STEP,),
        in_specs=in_specs,
        out_specs=whole(ROWS + TAIL),
        out_shape=jax.ShapeDtypeStruct((ROWS + TAIL, 128), BF16),
        scratch_shapes=scratch,
        compiler_params=pltpu.CompilerParams(
            dimension_semantics=("arbitrary",), vmem_limit_bytes=LIMIT
        ),
        cost_estimate=SMALL,
        name="attend_" + kind,
    )(*args)


def lines_of(tail):
    tail = tail.astype(F32)
    return tail[:BLOCKS] + tail[BLOCKS : 2 * BLOCKS] + tail[2 * BLOCKS : 3 * BLOCKS]


def mix(lines, b, on):
    first, second = lines[0][b : b + 1], jnp.where(on, lines[1][b : b + 1], F32(LOW))
    top = jnp.maximum(first, second)
    total = jnp.exp2(first - top) + jnp.exp2(second - top)
    eye = iota((128, 128), 0) == iota((128, 128), 1)
    share = jnp.exp2(second - top) / total
    column = jnp.sum(jnp.where(eye, share, F32(0)), axis=1, keepdims=True)
    return column, top + jnp.log2(total)


def mix_kernel(flags, own_ref, back_ref, here_ref, sum_ref, lines_ref):
    odd, chip = flags[0], flags[1]

    def run(other, on):
        lines = lines_of(own_ref[ROWS:]), lines_of(other[ROWS:])
        lines_ref[...] = jnp.zeros_like(lines_ref)
        for b in range(BLOCKS):
            rows = slice(b * 128, (b + 1) * 128)
            share, line = mix(lines, b, on)
            own = own_ref[rows].astype(F32)
            sum_ref[rows] = (own + share * (other[rows].astype(F32) - own)).astype(BF16)
            lines_ref[b : b + 1] = line

    pl.when(odd == 0)(lambda: run(back_ref, chip >= 1))
    pl.when(odd == 1)(lambda: run(here_ref, odd == 1))


def mix_early(flags, own, back, here):
    return pl.pallas_call(
        mix_kernel,
        in_specs=[pl.BlockSpec(memory_space=pltpu.SMEM)] + [pl.BlockSpec(memory_space=pltpu.VMEM)] * 3,
        out_shape=[jax.ShapeDtypeStruct((ROWS, 128), BF16), jax.ShapeDtypeStruct((LINES, 128), F32)],
        compiler_params=pltpu.CompilerParams(vmem_limit_bytes=24 * 2**20),
        cost_estimate=SMALL,
        name="mix_early",
    )(flags, own, back, here)


def finish_kernel(flags, sum_ref, lines_ref, near_ref, far_ref, slots_ref, out_ref, merged):
    odd, chip = flags[0], flags[1]

    def merge(late_ref, on):
        lines = lines_ref[:BLOCKS], lines_of(late_ref[ROWS:])
        for b in range(BLOCKS):
            rows = slice(b * 128, (b + 1) * 128)
            share, _ = mix(lines, b, on)
            early = sum_ref[rows].astype(F32)
            merged[rows] = (early + share * (late_ref[rows].astype(F32) - early)).astype(BF16)

    pl.when(odd == 1)(lambda: merge(near_ref, chip >= 1))
    pl.when(odd == 0)(lambda: merge(far_ref, chip >= 2))
    entries = out_ref.shape[0]
    for e in range(entries // 256):
        rows = slice(e * 256, (e + 1) * 256)
        place = one_hot(iota((256, ROWS), 1) == slots_ref[rows])
        out_ref[rows] = dot(place, merged[...]).astype(BF16)


def finish(flags, early, lines, near, far, slots_column):
    entries = slots_column.shape[0]
    return pl.pallas_call(
        finish_kernel,
        in_specs=[pl.BlockSpec(memory_space=pltpu.SMEM)] + [pl.BlockSpec(memory_space=pltpu.VMEM)] * 5,
        out_shape=jax.ShapeDtypeStruct((entries, 128), BF16),
        scratch_shapes=[pltpu.VMEM((ROWS, 128), BF16)],
        compiler_params=pltpu.CompilerParams(vmem_limit_bytes=24 * 2**20),
        cost_estimate=SMALL,
        name="finish",
    )(flags, early, lines, near, far, slots_column)


def moved(block, distance):
    devices = range(lax.axis_size("seq"))
    pairs = [(i, i + distance(i)) for i in devices if distance(i) and i + distance(i) in devices]
    return lax.ppermute(block, "seq", pairs)


def shards(queries, keys, values, routes):
    tokens, routed, width = queries.shape
    devices = range(lax.axis_size("seq"))
    device = lax.axis_index("seq").astype(I32)
    flags = jnp.stack([device % 2, device // 2])

    def after(x, *others):
        return lax.optimization_barrier((x, *others))[0]

    kv = jnp.stack([keys.transpose(1, 0, 2), values.transpose(1, 0, 2)])
    kv_forward = moved(kv, lambda i: 2 if i % 2 else 0)
    packed, pos, slots = sort_queries(after(routes.T, kv), queries.transpose(1, 0, 2).reshape(-1, width))
    column = slots.T.reshape(-1, 1)
    near_q = moved(packed, lambda i: -2)
    own = attend("own", flags, [packed], [kv], pos)
    pairs = [[i, i + 1] for i in range(0, lax.axis_size("seq"), 2)]
    chip_kv = lax.all_gather(kv, "seq", axis_index_groups=pairs)
    far_q = moved(after(packed, own, column), lambda i: 0 if i % 2 else -4)
    near_q = after(near_q, own)
    near_out = attend("near", flags, [near_q], [chip_kv, chip_kv, kv_forward])
    near_back = moved(near_out, lambda i: 2)
    far_q = after(far_q, near_out)
    far_out = attend("far", flags, [far_q, packed], [chip_kv, chip_kv])
    far_back = moved(far_out, lambda i: 0 if i % 2 else 4)
    early_sum, early_lines = mix_early(flags, own, near_back, far_out)
    out = finish(flags, early_sum, early_lines, near_back, after(far_back, early_sum), column)
    return out.reshape(tokens, routed, width)


def solution(mesh):
    placed = (P("seq", None, None), P("seq", None, None), P("seq", None, None), P("seq", None))
    return jax.shard_map(
        shards, mesh=mesh, in_specs=placed, out_specs=P("seq", None, None), check_vma=False
    )
```

```python
import functools

import jax
import jax.numpy as jnp
from jax import lax
from jax.experimental import pallas as pl
from jax.experimental.pallas import tpu as pltpu
from jax.sharding import PartitionSpec as P

GROUPS = 8
MOST_GROUP = 320
ROWS = 2176
SPAN = ROWS + MOST_GROUP
META = 16
TAIL = 64
BLOCKS = ROWS // 128
LINES = 24
CHUNK = 160
STEP = 4
LIMIT = 32 * 2**20
SMALL = pl.CostEstimate(flops=1000, bytes_accessed=1000, transcendentals=0)
LOW = -1e30
SCALE = 1.4426950408889634 / (128.0**0.5)
F32, BF16, I32 = jnp.float32, jnp.bfloat16, jnp.int32


def dot(a, b):
    return jnp.dot(a, b, preferred_element_type=F32)


def dot_t(a, b):
    return lax.dot_general(a, b, (((1,), (1,)), ((), ())), preferred_element_type=F32)


def iota(shape, dim):
    return lax.broadcasted_iota(I32, shape, dim)


def one_hot(mask):
    return jnp.where(mask, F32(1), F32(0)).astype(BF16)


def sort_kernel(routes_ref, q_ref, packed_ref, pos_ref, slots_ref, right):
    routed, tokens = routes_ref.shape
    entries = routed * tokens
    group = lax.shift_right_logical(routes_ref[...], 3)
    hot = jnp.concatenate([jnp.where(group == g, F32(1), F32(0)) for g in range(GROUPS)], axis=0)
    hot16 = hot.astype(BF16)
    before = dot(hot16, one_hot(iota((tokens, tokens), 0) < iota((tokens, tokens), 1)))
    total = dot(hot16, jnp.ones((tokens, tokens), BF16)).astype(BF16)
    side = (GROUPS * routed, GROUPS * routed)
    row, col = iota(side, 0), iota(side, 1)
    same = (row // routed) == (col // routed)
    earlier = dot(one_hot(same & (col < row)), total)
    count = dot(one_hot(same), total).astype(I32)
    sixteens = lax.shift_right_logical(count + 15, 4).astype(F32).astype(BF16)
    first = dot(one_hot(((col // routed) < (row // routed)) & (col % routed == 0)), sixteens)
    places = hot * (before + earlier + 16.0 * first)
    slots = sum(places[g * routed : (g + 1) * routed] for g in range(GROUPS)).astype(I32)
    slots_ref[...] = slots
    line = jnp.concatenate([slots[r : r + 1] for r in range(routed)], axis=1)
    right[:, :128] = q_ref[...]
    right[:, 128:] = (iota((entries, 128), 0) % tokens).astype(F32).astype(BF16)
    eye = iota((128, 128), 0) == iota((128, 128), 1)
    pos_ref[...] = jnp.zeros_like(pos_ref)
    for b in range(BLOCKS):
        place = one_hot(iota((128, entries), 0) + b * 128 == line)
        sorted_rows = dot(place, right[...])
        packed_ref[b * 128 : (b + 1) * 128] = sorted_rows[:, :128].astype(BF16)
        pos_ref[b : b + 1] = jnp.sum(jnp.where(eye, sorted_rows[:, 128:], F32(0)), axis=0, keepdims=True)
    starts = jnp.concatenate([first[g * routed : g * routed + 1, :128] for g in range(GROUPS)], axis=0)
    packed_ref[ROWS : ROWS + META] = jnp.concatenate([starts, jnp.zeros_like(starts)], axis=0).astype(BF16)


def sort_queries(routes_t, queries_r):
    routed, tokens = routes_t.shape
    return pl.pallas_call(
        sort_kernel,
        out_shape=[
            jax.ShapeDtypeStruct((ROWS + META, 128), BF16),
            jax.ShapeDtypeStruct((LINES, 128), F32),
            jax.ShapeDtypeStruct((routed, tokens), I32),
        ],
        scratch_shapes=[pltpu.VMEM((routed * tokens, 256), BF16)],
        compiler_params=pltpu.CompilerParams(vmem_limit_bytes=24 * 2**20),
        cost_estimate=SMALL,
        name="sort_queries",
    )(routes_t, queries_r)


def attend_kernel(kind, flags, q_ref, *refs):
    kv_count = {"own": 1, "near": 3, "far": 2}[kind]
    kv, refs = refs[:kv_count], refs[kv_count:]
    if kind == "own":
        pos_ref, out_ref, qs, os, ls, tail, starts, ps = refs
    else:
        out_ref, qs, os, ls, tail, starts = refs
    step = pl.program_id(0)
    odd, chip = flags[0], flags[1]

    def shard_parts(i, is_odd):
        if kind == "own":
            return [
                (kv[0][0, i, :256], kv[0][1, i, :256], None, False),
                (kv[0][0, i, 256:], kv[0][1, i, 256:], None, True),
            ]
        sibling = (kv[1][0, i], kv[1][1, i], None, False)
        if kind == "far" and is_odd:
            return [sibling]
        parts = [(kv[0][0, i], kv[0][1, i], None, False), sibling]
        if is_odd:
            flag = jnp.where(chip >= 1, F32(0), F32(LOW))
            parts.append((kv[2][0, i], kv[2][1, i], flag, False))
        return parts

    def work(is_odd):
        @pl.when(step == 0)
        def _():
            qs[: ROWS + META] = q_ref[...]
            os[...] = jnp.zeros_like(os)
            ls[...] = jnp.zeros_like(ls)
            firsts = qs[ROWS : ROWS + META].astype(F32)
            for g in range(GROUPS):
                starts[g] = jnp.max(firsts[g : g + 1]).astype(I32)
            if kind == "own":
                eye = iota((128, 128), 0) == iota((128, 128), 1)
                for b in range(BLOCKS):
                    picked = jnp.where(eye, pos_ref[b : b + 1], F32(0))
                    reach = jnp.sum(picked, axis=1, keepdims=True)
                    ps[b * 128 : (b + 1) * 128] = jnp.broadcast_to(reach, (128, 128))

        units = []
        for i in range(STEP):
            start = pl.multiple_of(starts[step * STEP + i] * 16, 16)
            parts = shard_parts(i, is_odd)
            for c in range(MOST_GROUP // CHUNK):
                units.append((pl.ds(pl.multiple_of(start + c * CHUNK, 16), CHUNK), parts))
        scored = []
        for rows, parts in units:
            q = qs[rows, :]
            scores = []
            for k, _, _, causal in parts:
                s = dot_t(q, k)
                if causal:
                    reach = ps[rows, :][:, :1]
                    s = jnp.where(iota(s.shape, 1).astype(F32) <= reach, s, F32(LOW))
                scores.append(s)
            scored.append(scores)
        tops = []
        for (rows, parts), scores in zip(units, scored):
            peaks = []
            for s, (_, _, bias, _) in zip(scores, parts):
                peak = jnp.max(s, axis=1, keepdims=True)
                peaks.append(peak if bias is None else peak + bias)
            tops.append(functools.reduce(jnp.maximum, peaks))
        results = []
        for (rows, parts), scores, top in zip(units, scored, tops):
            both = None
            for s, (_, v, bias, _) in zip(scores, parts):
                base = top if bias is None else top - bias
                weight = jnp.exp2((s - base) * F32(SCALE)).astype(BF16)
                product = dot(weight, jnp.concatenate([v, jnp.ones_like(v)], axis=1))
                both = product if both is None else both + product
            results.append(both)
        for (rows, parts), both, top in zip(units, results, tops):
            total = both[:, 128:]
            os[rows, :] = (both[:, :128] / total).astype(BF16)
            ls[rows, :] = top * F32(SCALE) + jnp.log2(total)

        @pl.when(step == GROUPS // STEP - 1)
        def _():
            out_ref[:ROWS] = os[:ROWS]
            eye = iota((128, 128), 0) == iota((128, 128), 1)
            tail[...] = jnp.zeros_like(tail)
            for b in range(BLOCKS):
                square = ls[b * 128 : (b + 1) * 128]
                line = jnp.sum(jnp.where(eye, square, F32(0)), axis=0, keepdims=True)
                high = line.astype(BF16).astype(F32)
                middle = (line - high).astype(BF16).astype(F32)
                tail[b : b + 1] = high
                tail[BLOCKS + b : BLOCKS + b + 1] = middle
                tail[2 * BLOCKS + b : 2 * BLOCKS + b + 1] = line - high - middle
            out_ref[ROWS:] = tail[...].astype(BF16)

    if kind == "own":
        work(False)
    else:
        pl.when(odd == 0)(lambda: work(False))
        pl.when(odd == 1)(lambda: work(True))


def attend(kind, flags, packed, kvs, pos=None):
    kv_spec = pl.BlockSpec((2, STEP, 512, 128), lambda g: (0, g, 0, 0))

    def whole(rows):
        return pl.BlockSpec((rows, 128), lambda g: (0, 0))

    in_specs = [pl.BlockSpec(memory_space=pltpu.SMEM)]
    in_specs += [whole(ROWS + META)] + [kv_spec] * len(kvs)
    args = [flags, packed, *kvs]
    scratch = [pltpu.VMEM((SPAN, 128), BF16), pltpu.VMEM((SPAN, 128), BF16), pltpu.VMEM((SPAN, 128), F32)]
    scratch += [pltpu.VMEM((TAIL, 128), F32), pltpu.SMEM((GROUPS,), I32)]
    if kind == "own":
        in_specs.append(whole(LINES))
        args.append(pos)
        scratch.append(pltpu.VMEM((SPAN, 128), F32))
    return pl.pallas_call(
        functools.partial(attend_kernel, kind),
        grid=(GROUPS // STEP,),
        in_specs=in_specs,
        out_specs=whole(ROWS + TAIL),
        out_shape=jax.ShapeDtypeStruct((ROWS + TAIL, 128), BF16),
        scratch_shapes=scratch,
        compiler_params=pltpu.CompilerParams(
            dimension_semantics=("arbitrary",), vmem_limit_bytes=LIMIT
        ),
        cost_estimate=SMALL,
        name="attend_" + kind,
    )(*args)


def lines_of(tail):
    tail = tail.astype(F32)
    return tail[:BLOCKS] + tail[BLOCKS : 2 * BLOCKS] + tail[2 * BLOCKS : 3 * BLOCKS]


def mix(lines, b, on):
    first, second = lines[0][b : b + 1], jnp.where(on, lines[1][b : b + 1], F32(LOW))
    top = jnp.maximum(first, second)
    total = jnp.exp2(first - top) + jnp.exp2(second - top)
    eye = iota((128, 128), 0) == iota((128, 128), 1)
    share = jnp.exp2(second - top) / total
    column = jnp.sum(jnp.where(eye, share, F32(0)), axis=1, keepdims=True)
    return column, top + jnp.log2(total)


def mix_kernel(flags, own_ref, back_ref, here_ref, sum_ref, lines_ref):
    odd, chip = flags[0], flags[1]

    def run(other, on):
        lines = lines_of(own_ref[ROWS:]), lines_of(other[ROWS:])
        lines_ref[...] = jnp.zeros_like(lines_ref)
        for b in range(BLOCKS):
            rows = slice(b * 128, (b + 1) * 128)
            share, line = mix(lines, b, on)
            own = own_ref[rows].astype(F32)
            sum_ref[rows] = (own + share * (other[rows].astype(F32) - own)).astype(BF16)
            lines_ref[b : b + 1] = line

    pl.when(odd == 0)(lambda: run(back_ref, chip >= 1))
    pl.when(odd == 1)(lambda: run(here_ref, odd == 1))


def mix_early(flags, own, back, here):
    return pl.pallas_call(
        mix_kernel,
        in_specs=[pl.BlockSpec(memory_space=pltpu.SMEM)] + [pl.BlockSpec(memory_space=pltpu.VMEM)] * 3,
        out_shape=[jax.ShapeDtypeStruct((ROWS, 128), BF16), jax.ShapeDtypeStruct((LINES, 128), F32)],
        compiler_params=pltpu.CompilerParams(vmem_limit_bytes=24 * 2**20),
        cost_estimate=SMALL,
        name="mix_early",
    )(flags, own, back, here)


def finish_kernel(flags, sum_ref, lines_ref, near_ref, far_ref, slots_ref, out_ref, merged):
    odd, chip = flags[0], flags[1]

    def merge(late_ref, on):
        lines = lines_ref[:BLOCKS], lines_of(late_ref[ROWS:])
        for b in range(BLOCKS):
            rows = slice(b * 128, (b + 1) * 128)
            share, _ = mix(lines, b, on)
            early = sum_ref[rows].astype(F32)
            merged[rows] = (early + share * (late_ref[rows].astype(F32) - early)).astype(BF16)

    pl.when(odd == 1)(lambda: merge(near_ref, chip >= 1))
    pl.when(odd == 0)(lambda: merge(far_ref, chip >= 2))
    entries = out_ref.shape[0]
    for e in range(entries // 256):
        rows = slice(e * 256, (e + 1) * 256)
        place = one_hot(iota((256, ROWS), 1) == slots_ref[rows])
        out_ref[rows] = dot(place, merged[...]).astype(BF16)


def finish(flags, early, lines, near, far, slots_column):
    entries = slots_column.shape[0]
    return pl.pallas_call(
        finish_kernel,
        in_specs=[pl.BlockSpec(memory_space=pltpu.SMEM)] + [pl.BlockSpec(memory_space=pltpu.VMEM)] * 5,
        out_shape=jax.ShapeDtypeStruct((entries, 128), BF16),
        scratch_shapes=[pltpu.VMEM((ROWS, 128), BF16)],
        compiler_params=pltpu.CompilerParams(vmem_limit_bytes=24 * 2**20),
        cost_estimate=SMALL,
        name="finish",
    )(flags, early, lines, near, far, slots_column)


def moved(block, distance):
    devices = range(lax.axis_size("seq"))
    pairs = [(i, i + distance(i)) for i in devices if distance(i) is not None and i + distance(i) in devices]
    return lax.ppermute(block, "seq", pairs)


def shards(queries, keys, values, routes):
    tokens, routed, width = queries.shape
    devices = range(lax.axis_size("seq"))
    device = lax.axis_index("seq").astype(I32)
    flags = jnp.stack([device % 2, device // 2])

    def after(x, *others):
        return lax.optimization_barrier((x, *others))[0]

    kv = jnp.stack([keys.transpose(1, 0, 2), values.transpose(1, 0, 2)])
    kv_forward = moved(kv, lambda i: 2 if i % 2 else None)
    packed, pos, slots = sort_queries(after(routes.T, kv), queries.transpose(1, 0, 2).reshape(-1, width))
    column = slots.T.reshape(-1, 1)
    near_q = moved(packed, lambda i: -2)
    own = attend("own", flags, packed, [kv], pos)
    kv_sibling = moved(kv, lambda i: -1 if i % 2 else 1)
    far_q = moved(after(packed, own, column), lambda i: 0 if i % 2 else -4)
    near_q = after(near_q, own)
    near_out = attend("near", flags, near_q, [kv, kv_sibling, kv_forward])
    near_back = moved(near_out, lambda i: 2)
    far_q = after(far_q, near_out)
    far_out = attend("far", flags, far_q, [kv, kv_sibling])
    far_back = moved(far_out, lambda i: None if i % 2 else 4)
    early_sum, early_lines = mix_early(flags, own, near_back, far_out)
    out = finish(flags, early_sum, early_lines, near_back, after(far_back, early_sum), column)
    return out.reshape(tokens, routed, width)


def solution(mesh):
    placed = (P("seq", None, None), P("seq", None, None), P("seq", None, None), P("seq", None))
    return jax.shard_map(
        shards, mesh=mesh, in_specs=placed, out_specs=P("seq", None, None), check_vma=False
    )
```

```python
import functools

import jax
import jax.numpy as jnp
from jax import lax
from jax.experimental import pallas as pl
from jax.experimental.pallas import tpu as pltpu
from jax.sharding import PartitionSpec as P

GROUPS = 8
MOST_GROUP = 320
ROWS = 2176
SPAN = ROWS + MOST_GROUP
META = 16
TAIL = 64
BLOCKS = ROWS // 128
LINES = 24
CHUNK = 160
STEP = 4
LIMIT = 32 * 2**20
SMALL = pl.CostEstimate(flops=1000, bytes_accessed=1000, transcendentals=0)
LOW = -1e30
SCALE = 1.4426950408889634 / (128.0**0.5)
F32, BF16, I32 = jnp.float32, jnp.bfloat16, jnp.int32


def dot(a, b):
    return jnp.dot(a, b, preferred_element_type=F32)


def dot_t(a, b):
    return lax.dot_general(a, b, (((1,), (1,)), ((), ())), preferred_element_type=F32)


def iota(shape, dim):
    return lax.broadcasted_iota(I32, shape, dim)


def one_hot(mask):
    return jnp.where(mask, F32(1), F32(0)).astype(BF16)


def sort_kernel(routes_ref, q_ref, packed_ref, pos_ref, slots_ref, right):
    routed, tokens = routes_ref.shape
    entries = routed * tokens
    group = lax.shift_right_logical(routes_ref[...], 3)
    hot = jnp.concatenate([jnp.where(group == g, F32(1), F32(0)) for g in range(GROUPS)], axis=0)
    hot16 = hot.astype(BF16)
    before = dot(hot16, one_hot(iota((tokens, tokens), 0) < iota((tokens, tokens), 1)))
    total = dot(hot16, jnp.ones((tokens, tokens), BF16)).astype(BF16)
    side = (GROUPS * routed, GROUPS * routed)
    row, col = iota(side, 0), iota(side, 1)
    same = (row // routed) == (col // routed)
    earlier = dot(one_hot(same & (col < row)), total)
    count = dot(one_hot(same), total).astype(I32)
    sixteens = lax.shift_right_logical(count + 15, 4).astype(F32).astype(BF16)
    first = dot(one_hot(((col // routed) < (row // routed)) & (col % routed == 0)), sixteens)
    places = hot * (before + earlier + 16.0 * first)
    slots = sum(places[g * routed : (g + 1) * routed] for g in range(GROUPS)).astype(I32)
    slots_ref[...] = slots
    line = jnp.concatenate([slots[r : r + 1] for r in range(routed)], axis=1)
    right[:, :128] = q_ref[...]
    right[:, 128:] = (iota((entries, 128), 0) % tokens).astype(F32).astype(BF16)
    eye = iota((128, 128), 0) == iota((128, 128), 1)
    pos_ref[...] = jnp.zeros_like(pos_ref)
    for b in range(BLOCKS):
        place = one_hot(iota((128, entries), 0) + b * 128 == line)
        sorted_rows = dot(place, right[...])
        packed_ref[b * 128 : (b + 1) * 128] = sorted_rows[:, :128].astype(BF16)
        pos_ref[b : b + 1] = jnp.sum(jnp.where(eye, sorted_rows[:, 128:], F32(0)), axis=0, keepdims=True)
    starts = jnp.concatenate([first[g * routed : g * routed + 1, :128] for g in range(GROUPS)], axis=0)
    packed_ref[ROWS : ROWS + META] = jnp.concatenate([starts, jnp.zeros_like(starts)], axis=0).astype(BF16)


def sort_queries(routes_t, queries_r):
    routed, tokens = routes_t.shape
    return pl.pallas_call(
        sort_kernel,
        out_shape=[
            jax.ShapeDtypeStruct((ROWS + META, 128), BF16),
            jax.ShapeDtypeStruct((LINES, 128), F32),
            jax.ShapeDtypeStruct((routed, tokens), I32),
        ],
        scratch_shapes=[pltpu.VMEM((routed * tokens, 256), BF16)],
        compiler_params=pltpu.CompilerParams(vmem_limit_bytes=24 * 2**20),
        cost_estimate=SMALL,
        name="sort_queries",
    )(routes_t, queries_r)


def attend_kernel(kind, flags, q_ref, *refs):
    kv_count = {"own": 1, "near": 3, "far": 2}[kind]
    kv, refs = refs[:kv_count], refs[kv_count:]
    if kind == "own":
        pos_ref, out_ref, qs, os, ls, tail, starts, ps = refs
    else:
        out_ref, qs, os, ls, tail, starts = refs
    step = pl.program_id(0)
    odd, chip = flags[0], flags[1]

    def shard_parts(i, is_odd):
        if kind == "own":
            return [
                (kv[0][0, i, :256], kv[0][1, i, :256], None, False),
                (kv[0][0, i, 256:], kv[0][1, i, 256:], None, True),
            ]
        sibling = (kv[1][0, i], kv[1][1, i], None, False)
        if kind == "far" and is_odd:
            return [sibling]
        parts = [(kv[0][0, i], kv[0][1, i], None, False), sibling]
        if is_odd:
            flag = jnp.where(chip >= 1, F32(0), F32(LOW))
            parts.append((kv[2][0, i], kv[2][1, i], flag, False))
        return parts

    def work(is_odd):
        @pl.when(step == 0)
        def _():
            qs[: ROWS + META] = q_ref[...]
            os[...] = jnp.zeros_like(os)
            ls[...] = jnp.zeros_like(ls)
            firsts = qs[ROWS : ROWS + META].astype(F32)
            for g in range(GROUPS):
                starts[g] = jnp.max(firsts[g : g + 1]).astype(I32)
            if kind == "own":
                eye = iota((128, 128), 0) == iota((128, 128), 1)
                for b in range(BLOCKS):
                    picked = jnp.where(eye, pos_ref[b : b + 1], F32(0))
                    reach = jnp.sum(picked, axis=1, keepdims=True)
                    ps[b * 128 : (b + 1) * 128] = jnp.broadcast_to(reach, (128, 128))

        units = []
        for i in range(STEP):
            start = pl.multiple_of(starts[step * STEP + i] * 16, 16)
            parts = shard_parts(i, is_odd)
            for c in range(MOST_GROUP // CHUNK):
                units.append((pl.ds(pl.multiple_of(start + c * CHUNK, 16), CHUNK), parts))
        scored = []
        for rows, parts in units:
            q = qs[rows, :]
            scores = []
            for k, _, _, causal in parts:
                s = dot_t(q, k)
                if causal:
                    reach = ps[rows, :][:, :1]
                    s = jnp.where(iota(s.shape, 1).astype(F32) <= reach, s, F32(LOW))
                scores.append(s)
            scored.append(scores)
        tops = []
        for (rows, parts), scores in zip(units, scored):
            peaks = []
            for s, (_, _, bias, _) in zip(scores, parts):
                peak = jnp.max(s, axis=1, keepdims=True)
                peaks.append(peak if bias is None else peak + bias)
            tops.append(functools.reduce(jnp.maximum, peaks))
        results = []
        for (rows, parts), scores, top in zip(units, scored, tops):
            both = None
            for s, (_, v, bias, _) in zip(scores, parts):
                base = top if bias is None else top - bias
                weight = jnp.exp2((s - base) * F32(SCALE)).astype(BF16)
                product = dot(weight, jnp.concatenate([v, jnp.ones_like(v)], axis=1))
                both = product if both is None else both + product
            results.append(both)
        for (rows, parts), both, top in zip(units, results, tops):
            total = both[:, 128:]
            os[rows, :] = (both[:, :128] / total).astype(BF16)
            ls[rows, :] = top * F32(SCALE) + jnp.log2(total)

        @pl.when(step == GROUPS // STEP - 1)
        def _():
            out_ref[:ROWS] = os[:ROWS]
            eye = iota((128, 128), 0) == iota((128, 128), 1)
            tail[...] = jnp.zeros_like(tail)
            for b in range(BLOCKS):
                square = ls[b * 128 : (b + 1) * 128]
                line = jnp.sum(jnp.where(eye, square, F32(0)), axis=0, keepdims=True)
                high = line.astype(BF16).astype(F32)
                middle = (line - high).astype(BF16).astype(F32)
                tail[b : b + 1] = high
                tail[BLOCKS + b : BLOCKS + b + 1] = middle
                tail[2 * BLOCKS + b : 2 * BLOCKS + b + 1] = line - high - middle
            out_ref[ROWS:] = tail[...].astype(BF16)

    if kind == "own":
        work(False)
    else:
        pl.when(odd == 0)(lambda: work(False))
        pl.when(odd == 1)(lambda: work(True))


def attend(kind, flags, packed, kvs, pos=None):
    kv_spec = pl.BlockSpec((2, STEP, 512, 128), lambda g: (0, g, 0, 0))

    def whole(rows):
        return pl.BlockSpec((rows, 128), lambda g: (0, 0))

    in_specs = [pl.BlockSpec(memory_space=pltpu.SMEM)]
    in_specs += [whole(ROWS + META)] + [kv_spec] * len(kvs)
    args = [flags, packed, *kvs]
    scratch = [pltpu.VMEM((SPAN, 128), BF16), pltpu.VMEM((SPAN, 128), BF16), pltpu.VMEM((SPAN, 128), F32)]
    scratch += [pltpu.VMEM((TAIL, 128), F32), pltpu.SMEM((GROUPS,), I32)]
    if kind == "own":
        in_specs.append(whole(LINES))
        args.append(pos)
        scratch.append(pltpu.VMEM((SPAN, 128), F32))
    return pl.pallas_call(
        functools.partial(attend_kernel, kind),
        grid=(GROUPS // STEP,),
        in_specs=in_specs,
        out_specs=whole(ROWS + TAIL),
        out_shape=jax.ShapeDtypeStruct((ROWS + TAIL, 128), BF16),
        scratch_shapes=scratch,
        compiler_params=pltpu.CompilerParams(
            dimension_semantics=("arbitrary",), vmem_limit_bytes=LIMIT
        ),
        cost_estimate=SMALL,
        name="attend_" + kind,
    )(*args)


def lines_of(tail):
    tail = tail.astype(F32)
    return tail[:BLOCKS] + tail[BLOCKS : 2 * BLOCKS] + tail[2 * BLOCKS : 3 * BLOCKS]


def mix(lines, b, on):
    first, second = lines[0][b : b + 1], jnp.where(on, lines[1][b : b + 1], F32(LOW))
    top = jnp.maximum(first, second)
    total = jnp.exp2(first - top) + jnp.exp2(second - top)
    eye = iota((128, 128), 0) == iota((128, 128), 1)
    share = jnp.exp2(second - top) / total
    column = jnp.sum(jnp.where(eye, share, F32(0)), axis=1, keepdims=True)
    return column, top + jnp.log2(total)


def mix_kernel(flags, own_ref, back_ref, here_ref, sum_ref, lines_ref):
    odd, chip = flags[0], flags[1]

    def run(other, on):
        lines = lines_of(own_ref[ROWS:]), lines_of(other[ROWS:])
        lines_ref[...] = jnp.zeros_like(lines_ref)
        for b in range(BLOCKS):
            rows = slice(b * 128, (b + 1) * 128)
            share, line = mix(lines, b, on)
            own = own_ref[rows].astype(F32)
            sum_ref[rows] = (own + share * (other[rows].astype(F32) - own)).astype(BF16)
            lines_ref[b : b + 1] = line

    pl.when(odd == 0)(lambda: run(back_ref, chip >= 1))
    pl.when(odd == 1)(lambda: run(here_ref, odd == 1))


def mix_early(flags, own, back, here):
    return pl.pallas_call(
        mix_kernel,
        in_specs=[pl.BlockSpec(memory_space=pltpu.SMEM)] + [pl.BlockSpec(memory_space=pltpu.VMEM)] * 3,
        out_shape=[jax.ShapeDtypeStruct((ROWS, 128), BF16), jax.ShapeDtypeStruct((LINES, 128), F32)],
        compiler_params=pltpu.CompilerParams(vmem_limit_bytes=24 * 2**20),
        cost_estimate=SMALL,
        name="mix_early",
    )(flags, own, back, here)


def finish_kernel(flags, sum_ref, lines_ref, near_ref, far_ref, slots_ref, out_ref, merged):
    odd, chip = flags[0], flags[1]

    def merge(late_ref, on):
        lines = lines_ref[:BLOCKS], lines_of(late_ref[ROWS:])
        for b in range(BLOCKS):
            rows = slice(b * 128, (b + 1) * 128)
            share, _ = mix(lines, b, on)
            early = sum_ref[rows].astype(F32)
            merged[rows] = (early + share * (late_ref[rows].astype(F32) - early)).astype(BF16)

    pl.when(odd == 1)(lambda: merge(near_ref, chip >= 1))
    pl.when(odd == 0)(lambda: merge(far_ref, chip >= 2))
    entries = out_ref.shape[0]
    for e in range(entries // 512):
        rows = slice(e * 512, (e + 1) * 512)
        place = one_hot(iota((512, ROWS), 1) == slots_ref[rows])
        out_ref[rows] = dot(place, merged[...]).astype(BF16)


def finish(flags, early, lines, near, far, slots_column):
    entries = slots_column.shape[0]
    return pl.pallas_call(
        finish_kernel,
        in_specs=[pl.BlockSpec(memory_space=pltpu.SMEM)] + [pl.BlockSpec(memory_space=pltpu.VMEM)] * 5,
        out_shape=jax.ShapeDtypeStruct((entries, 128), BF16),
        scratch_shapes=[pltpu.VMEM((ROWS, 128), BF16)],
        compiler_params=pltpu.CompilerParams(vmem_limit_bytes=24 * 2**20),
        cost_estimate=SMALL,
        name="finish",
    )(flags, early, lines, near, far, slots_column)


def moved(block, distance):
    devices = range(lax.axis_size("seq"))
    pairs = [(i, i + distance(i)) for i in devices if distance(i) is not None and i + distance(i) in devices]
    return lax.ppermute(block, "seq", pairs)


def shards(queries, keys, values, routes):
    tokens, routed, width = queries.shape
    devices = range(lax.axis_size("seq"))
    device = lax.axis_index("seq").astype(I32)
    flags = jnp.stack([device % 2, device // 2])

    def after(x, *others):
        return lax.optimization_barrier((x, *others))[0]

    kv = jnp.stack([keys.transpose(1, 0, 2), values.transpose(1, 0, 2)])
    kv_forward = moved(kv, lambda i: 2 if i % 2 else None)
    packed, pos, slots = sort_queries(after(routes.T, kv), queries.transpose(1, 0, 2).reshape(-1, width))
    column = slots.T.reshape(-1, 1)
    near_q = moved(packed, lambda i: -2)
    own = attend("own", flags, packed, [kv], pos)
    kv_sibling = moved(kv, lambda i: -1 if i % 2 else 1)
    far_q = moved(after(packed, own, column), lambda i: 0 if i % 2 else -4)
    near_q = after(near_q, own)
    near_out = attend("near", flags, near_q, [kv, kv_sibling, kv_forward])
    near_back = moved(near_out, lambda i: 2)
    far_q = after(far_q, near_out)
    far_out = attend("far", flags, far_q, [kv, kv_sibling])
    far_back = moved(far_out, lambda i: None if i % 2 else 4)
    early_sum, early_lines = mix_early(flags, own, near_back, far_out)
    out = finish(flags, early_sum, early_lines, near_back, after(far_back, early_sum), column)
    return out.reshape(tokens, routed, width)


def solution(mesh):
    placed = (P("seq", None, None), P("seq", None, None), P("seq", None, None), P("seq", None))
    return jax.shard_map(
        shards, mesh=mesh, in_specs=placed, out_specs=P("seq", None, None), check_vma=False
    )
```

```python
import functools

import jax
import jax.numpy as jnp
from jax import lax
from jax.experimental import pallas as pl
from jax.experimental.pallas import tpu as pltpu
from jax.sharding import PartitionSpec as P

GROUPS = 8
MOST_GROUP = 320
ROWS = 2176
SPAN = ROWS + MOST_GROUP
META = 16
TAIL = 64
BLOCKS = ROWS // 128
LINES = 24
CHUNK = 160
STEP = 4
LIMIT = 32 * 2**20
SMALL = pl.CostEstimate(flops=1000, bytes_accessed=1000, transcendentals=0)
LOW = -1e30
SCALE = 1.4426950408889634 / (128.0**0.5)
F32, BF16, I32 = jnp.float32, jnp.bfloat16, jnp.int32


def dot(a, b):
    return jnp.dot(a, b, preferred_element_type=F32)


def dot_t(a, b):
    return lax.dot_general(a, b, (((1,), (1,)), ((), ())), preferred_element_type=F32)


def iota(shape, dim):
    return lax.broadcasted_iota(I32, shape, dim)


def one_hot(mask):
    return jnp.where(mask, F32(1), F32(0)).astype(BF16)


def sort_kernel(routes_ref, q_ref, packed_ref, pos_ref, slots_ref, right):
    routed, tokens = routes_ref.shape
    entries = routed * tokens
    group = lax.shift_right_logical(routes_ref[...], 3)
    hot = jnp.concatenate([jnp.where(group == g, F32(1), F32(0)) for g in range(GROUPS)], axis=0)
    hot16 = hot.astype(BF16)
    before = dot(hot16, one_hot(iota((tokens, tokens), 0) < iota((tokens, tokens), 1)))
    total = dot(hot16, jnp.ones((tokens, tokens), BF16)).astype(BF16)
    side = (GROUPS * routed, GROUPS * routed)
    row, col = iota(side, 0), iota(side, 1)
    same = (row // routed) == (col // routed)
    earlier = dot(one_hot(same & (col < row)), total)
    count = dot(one_hot(same), total).astype(I32)
    sixteens = lax.shift_right_logical(count + 15, 4).astype(F32).astype(BF16)
    first = dot(one_hot(((col // routed) < (row // routed)) & (col % routed == 0)), sixteens)
    places = hot * (before + earlier + 16.0 * first)
    slots = sum(places[g * routed : (g + 1) * routed] for g in range(GROUPS)).astype(I32)
    slots_ref[...] = slots
    line = jnp.concatenate([slots[r : r + 1] for r in range(routed)], axis=1)
    right[:, :128] = q_ref[...]
    right[:, 128:] = (iota((entries, 128), 0) % tokens).astype(F32).astype(BF16)
    eye = iota((128, 128), 0) == iota((128, 128), 1)
    pos_ref[...] = jnp.zeros_like(pos_ref)
    for b in range(BLOCKS):
        place = one_hot(iota((128, entries), 0) + b * 128 == line)
        sorted_rows = dot(place, right[...])
        packed_ref[b * 128 : (b + 1) * 128] = sorted_rows[:, :128].astype(BF16)
        pos_ref[b : b + 1] = jnp.sum(jnp.where(eye, sorted_rows[:, 128:], F32(0)), axis=0, keepdims=True)
    starts = jnp.concatenate([first[g * routed : g * routed + 1, :128] for g in range(GROUPS)], axis=0)
    packed_ref[ROWS : ROWS + META] = jnp.concatenate([starts, jnp.zeros_like(starts)], axis=0).astype(BF16)


def sort_queries(routes_t, queries_r):
    routed, tokens = routes_t.shape
    return pl.pallas_call(
        sort_kernel,
        out_shape=[
            jax.ShapeDtypeStruct((ROWS + META, 128), BF16),
            jax.ShapeDtypeStruct((LINES, 128), F32),
            jax.ShapeDtypeStruct((routed, tokens), I32),
        ],
        scratch_shapes=[pltpu.VMEM((routed * tokens, 256), BF16)],
        compiler_params=pltpu.CompilerParams(vmem_limit_bytes=24 * 2**20),
        cost_estimate=SMALL,
        name="sort_queries",
    )(routes_t, queries_r)


def attend_kernel(kind, flags, q_ref, *refs):
    kv_count = {"own": 1, "near": 3, "far": 2}[kind]
    kv, refs = refs[:kv_count], refs[kv_count:]
    if kind == "own":
        pos_ref, out_ref, qs, os, ls, tail, starts, ps = refs
    else:
        out_ref, qs, os, ls, tail, starts = refs
    step = pl.program_id(0)
    odd, chip = flags[0], flags[1]

    def shard_parts(i, is_odd):
        if kind == "own":
            return [
                (kv[0][0, i, :256], kv[0][1, i, :256], None, False),
                (kv[0][0, i, 256:], kv[0][1, i, 256:], None, True),
            ]
        sibling = (kv[1][0, i], kv[1][1, i], None, False)
        if kind == "far" and is_odd:
            return [sibling]
        parts = [(kv[0][0, i], kv[0][1, i], None, False), sibling]
        if is_odd:
            flag = jnp.where(chip >= 1, F32(0), F32(LOW))
            parts.append((kv[2][0, i], kv[2][1, i], flag, False))
        return parts

    def work(is_odd):
        @pl.when(step == 0)
        def _():
            qs[: ROWS + META] = q_ref[...]
            os[...] = jnp.zeros_like(os)
            ls[...] = jnp.zeros_like(ls)
            firsts = qs[ROWS : ROWS + META].astype(F32)
            for g in range(GROUPS):
                starts[g] = jnp.max(firsts[g : g + 1]).astype(I32)
            if kind == "own":
                eye = iota((128, 128), 0) == iota((128, 128), 1)
                for b in range(BLOCKS):
                    picked = jnp.where(eye, pos_ref[b : b + 1], F32(0))
                    reach = jnp.sum(picked, axis=1, keepdims=True)
                    ps[b * 128 : (b + 1) * 128] = jnp.broadcast_to(reach, (128, 128))

        units = []
        for i in range(STEP):
            start = pl.multiple_of(starts[step * STEP + i] * 16, 16)
            parts = shard_parts(i, is_odd)
            for c in range(MOST_GROUP // CHUNK):
                units.append((pl.ds(pl.multiple_of(start + c * CHUNK, 16), CHUNK), parts))
        scored = []
        for rows, parts in units:
            q = qs[rows, :]
            scores = []
            for k, _, _, causal in parts:
                s = dot_t(q, k)
                if causal:
                    reach = ps[rows, :][:, :1]
                    s = jnp.where(iota(s.shape, 1).astype(F32) <= reach, s, F32(LOW))
                scores.append(s)
            scored.append(scores)
        tops = []
        for (rows, parts), scores in zip(units, scored):
            peaks = []
            for s, (_, _, bias, _) in zip(scores, parts):
                peak = jnp.max(s, axis=1, keepdims=True)
                peaks.append(peak if bias is None else peak + bias)
            tops.append(functools.reduce(jnp.maximum, peaks))
        results = []
        for (rows, parts), scores, top in zip(units, scored, tops):
            both = None
            for s, (_, v, bias, _) in zip(scores, parts):
                base = top if bias is None else top - bias
                weight = jnp.exp2((s - base) * F32(SCALE)).astype(BF16)
                product = dot(weight, jnp.concatenate([v, jnp.ones_like(v)], axis=1))
                both = product if both is None else both + product
            results.append(both)
        for (rows, parts), both, top in zip(units, results, tops):
            total = both[:, 128:]
            os[rows, :] = (both[:, :128] / total).astype(BF16)
            ls[rows, :] = top * F32(SCALE) + jnp.log2(total)

        @pl.when(step == GROUPS // STEP - 1)
        def _():
            out_ref[:ROWS] = os[:ROWS]
            eye = iota((128, 128), 0) == iota((128, 128), 1)
            tail[...] = jnp.zeros_like(tail)
            for b in range(BLOCKS):
                square = ls[b * 128 : (b + 1) * 128]
                line = jnp.sum(jnp.where(eye, square, F32(0)), axis=0, keepdims=True)
                high = line.astype(BF16).astype(F32)
                middle = (line - high).astype(BF16).astype(F32)
                tail[b : b + 1] = high
                tail[BLOCKS + b : BLOCKS + b + 1] = middle
                tail[2 * BLOCKS + b : 2 * BLOCKS + b + 1] = line - high - middle
            out_ref[ROWS:] = tail[...].astype(BF16)

    if kind == "own":
        work(False)
    else:
        pl.when(odd == 0)(lambda: work(False))
        pl.when(odd == 1)(lambda: work(True))


def attend(kind, flags, packed, kvs, pos=None):
    kv_spec = pl.BlockSpec((2, STEP, 512, 128), lambda g: (0, g, 0, 0))

    def whole(rows):
        return pl.BlockSpec((rows, 128), lambda g: (0, 0))

    in_specs = [pl.BlockSpec(memory_space=pltpu.SMEM)]
    in_specs += [whole(ROWS + META)] + [kv_spec] * len(kvs)
    args = [flags, packed, *kvs]
    scratch = [pltpu.VMEM((SPAN, 128), BF16), pltpu.VMEM((SPAN, 128), BF16), pltpu.VMEM((SPAN, 128), F32)]
    scratch += [pltpu.VMEM((TAIL, 128), F32), pltpu.SMEM((GROUPS,), I32)]
    if kind == "own":
        in_specs.append(whole(LINES))
        args.append(pos)
        scratch.append(pltpu.VMEM((SPAN, 128), F32))
    return pl.pallas_call(
        functools.partial(attend_kernel, kind),
        grid=(GROUPS // STEP,),
        in_specs=in_specs,
        out_specs=whole(ROWS + TAIL),
        out_shape=jax.ShapeDtypeStruct((ROWS + TAIL, 128), BF16),
        scratch_shapes=scratch,
        compiler_params=pltpu.CompilerParams(
            dimension_semantics=("arbitrary",), vmem_limit_bytes=LIMIT
        ),
        cost_estimate=SMALL,
        name="attend_" + kind,
    )(*args)


def lines_of(tail):
    tail = tail.astype(F32)
    return tail[:BLOCKS] + tail[BLOCKS : 2 * BLOCKS] + tail[2 * BLOCKS : 3 * BLOCKS]


def mix(lines, b, on):
    first, second = lines[0][b : b + 1], jnp.where(on, lines[1][b : b + 1], F32(LOW))
    top = jnp.maximum(first, second)
    total = jnp.exp2(first - top) + jnp.exp2(second - top)
    eye = iota((128, 128), 0) == iota((128, 128), 1)
    share = jnp.exp2(second - top) / total
    column = jnp.sum(jnp.where(eye, share, F32(0)), axis=1, keepdims=True)
    return column, top + jnp.log2(total)


def mix_kernel(flags, own_ref, back_ref, here_ref, sum_ref, lines_ref):
    odd, chip = flags[0], flags[1]

    def run(other, on):
        lines = lines_of(own_ref[ROWS:]), lines_of(other[ROWS:])
        lines_ref[...] = jnp.zeros_like(lines_ref)
        for b in range(BLOCKS):
            rows = slice(b * 128, (b + 1) * 128)
            share, line = mix(lines, b, on)
            own = own_ref[rows].astype(F32)
            sum_ref[rows] = (own + share * (other[rows].astype(F32) - own)).astype(BF16)
            lines_ref[b : b + 1] = line

    pl.when(odd == 0)(lambda: run(back_ref, chip >= 1))
    pl.when(odd == 1)(lambda: run(here_ref, odd == 1))


def mix_early(flags, own, back, here):
    return pl.pallas_call(
        mix_kernel,
        in_specs=[pl.BlockSpec(memory_space=pltpu.SMEM)] + [pl.BlockSpec(memory_space=pltpu.VMEM)] * 3,
        out_shape=[jax.ShapeDtypeStruct((ROWS, 128), BF16), jax.ShapeDtypeStruct((LINES, 128), F32)],
        compiler_params=pltpu.CompilerParams(vmem_limit_bytes=24 * 2**20),
        cost_estimate=SMALL,
        name="mix_early",
    )(flags, own, back, here)


def finish_kernel(flags, sum_ref, lines_ref, near_ref, far_ref, slots_ref, out_ref, merged):
    odd, chip = flags[0], flags[1]

    def merge(late_ref, on):
        lines = lines_ref[:BLOCKS], lines_of(late_ref[ROWS:])
        for b in range(BLOCKS):
            rows = slice(b * 128, (b + 1) * 128)
            share, _ = mix(lines, b, on)
            early = sum_ref[rows].astype(F32)
            merged[rows] = (early + share * (late_ref[rows].astype(F32) - early)).astype(BF16)

    pl.when(odd == 1)(lambda: merge(near_ref, chip >= 1))
    pl.when(odd == 0)(lambda: merge(far_ref, chip >= 2))
    entries = out_ref.shape[0]
    for e in range(entries // 256):
        rows = slice(e * 256, (e + 1) * 256)
        place = one_hot(iota((256, ROWS), 1) == slots_ref[rows])
        out_ref[rows] = dot(place, merged[...]).astype(BF16)


def finish(flags, early, lines, near, far, slots_column):
    entries = slots_column.shape[0]
    return pl.pallas_call(
        finish_kernel,
        in_specs=[pl.BlockSpec(memory_space=pltpu.SMEM)] + [pl.BlockSpec(memory_space=pltpu.VMEM)] * 5,
        out_shape=jax.ShapeDtypeStruct((entries, 128), BF16),
        scratch_shapes=[pltpu.VMEM((ROWS, 128), BF16)],
        compiler_params=pltpu.CompilerParams(vmem_limit_bytes=24 * 2**20),
        cost_estimate=SMALL,
        name="finish",
    )(flags, early, lines, near, far, slots_column)


def moved(block, distance):
    devices = range(lax.axis_size("seq"))
    pairs = [(i, i + distance(i)) for i in devices if distance(i) is not None and i + distance(i) in devices]
    return lax.ppermute(block, "seq", pairs)


def shards(queries, keys, values, routes):
    tokens, routed, width = queries.shape
    devices = range(lax.axis_size("seq"))
    device = lax.axis_index("seq").astype(I32)
    flags = jnp.stack([device % 2, device // 2])

    def after(x, *others):
        return lax.optimization_barrier((x, *others))[0]

    kv = jnp.stack([keys.transpose(1, 0, 2), values.transpose(1, 0, 2)])
    kv_forward = moved(kv, lambda i: 2 if i % 2 else None)
    packed, pos, slots = sort_queries(after(routes.T, kv), queries.transpose(1, 0, 2).reshape(-1, width))
    column = slots.T.reshape(-1, 1)
    near_q = moved(packed, lambda i: -2)
    own = attend("own", flags, packed, [kv], pos)
    kv_sibling = moved(kv, lambda i: -1 if i % 2 else 1)
    far_q = moved(packed, lambda i: 0 if i % 2 else -4)
    near_q = after(near_q, own)
    near_out = attend("near", flags, near_q, [kv, kv_sibling, kv_forward])
    near_back = moved(near_out, lambda i: 2)
    far_q = after(far_q, near_out)
    far_out = attend("far", flags, far_q, [kv, kv_sibling])
    far_back = moved(far_out, lambda i: None if i % 2 else 4)
    early_sum, early_lines = mix_early(flags, own, near_back, far_out)
    out = finish(flags, early_sum, early_lines, near_back, after(far_back, early_sum), column)
    return out.reshape(tokens, routed, width)


def solution(mesh):
    placed = (P("seq", None, None), P("seq", None, None), P("seq", None, None), P("seq", None))
    return jax.shard_map(
        shards, mesh=mesh, in_specs=placed, out_specs=P("seq", None, None), check_vma=False
    )
```

```python
import functools

import jax
import jax.numpy as jnp
from jax import lax
from jax.experimental import pallas as pl
from jax.experimental.pallas import tpu as pltpu
from jax.sharding import PartitionSpec as P

GROUPS = 8
MOST_GROUP = 320
ROWS = 2176
SPAN = ROWS + MOST_GROUP
META = 16
TAIL = 64
BLOCKS = ROWS // 128
LINES = 24
CHUNK = 160
STEP = 8
LIMIT = 44 * 2**20
SMALL = pl.CostEstimate(flops=1000, bytes_accessed=1000, transcendentals=0)
LOW = -1e30
SCALE = 1.4426950408889634 / (128.0**0.5)
F32, BF16, I32 = jnp.float32, jnp.bfloat16, jnp.int32


def dot(a, b):
    return jnp.dot(a, b, preferred_element_type=F32)


def dot_t(a, b):
    return lax.dot_general(a, b, (((1,), (1,)), ((), ())), preferred_element_type=F32)


def iota(shape, dim):
    return lax.broadcasted_iota(I32, shape, dim)


def one_hot(mask):
    return jnp.where(mask, F32(1), F32(0)).astype(BF16)


def sort_kernel(routes_ref, q_ref, packed_ref, pos_ref, slots_ref, right):
    routed, tokens = routes_ref.shape
    entries = routed * tokens
    group = lax.shift_right_logical(routes_ref[...], 3)
    hot = jnp.concatenate([jnp.where(group == g, F32(1), F32(0)) for g in range(GROUPS)], axis=0)
    hot16 = hot.astype(BF16)
    before = dot(hot16, one_hot(iota((tokens, tokens), 0) < iota((tokens, tokens), 1)))
    total = dot(hot16, jnp.ones((tokens, tokens), BF16)).astype(BF16)
    side = (GROUPS * routed, GROUPS * routed)
    row, col = iota(side, 0), iota(side, 1)
    same = (row // routed) == (col // routed)
    earlier = dot(one_hot(same & (col < row)), total)
    count = dot(one_hot(same), total).astype(I32)
    sixteens = lax.shift_right_logical(count + 15, 4).astype(F32).astype(BF16)
    first = dot(one_hot(((col // routed) < (row // routed)) & (col % routed == 0)), sixteens)
    places = hot * (before + earlier + 16.0 * first)
    slots = sum(places[g * routed : (g + 1) * routed] for g in range(GROUPS)).astype(I32)
    slots_ref[...] = slots
    line = jnp.concatenate([slots[r : r + 1] for r in range(routed)], axis=1)
    right[:, :128] = q_ref[...]
    right[:, 128:] = (iota((entries, 128), 0) % tokens).astype(F32).astype(BF16)
    eye = iota((128, 128), 0) == iota((128, 128), 1)
    pos_ref[...] = jnp.zeros_like(pos_ref)
    for b in range(BLOCKS):
        place = one_hot(iota((128, entries), 0) + b * 128 == line)
        sorted_rows = dot(place, right[...])
        packed_ref[b * 128 : (b + 1) * 128] = sorted_rows[:, :128].astype(BF16)
        pos_ref[b : b + 1] = jnp.sum(jnp.where(eye, sorted_rows[:, 128:], F32(0)), axis=0, keepdims=True)
    starts = jnp.concatenate([first[g * routed : g * routed + 1, :128] for g in range(GROUPS)], axis=0)
    packed_ref[ROWS : ROWS + META] = jnp.concatenate([starts, jnp.zeros_like(starts)], axis=0).astype(BF16)


def sort_queries(routes_t, queries_r):
    routed, tokens = routes_t.shape
    return pl.pallas_call(
        sort_kernel,
        out_shape=[
            jax.ShapeDtypeStruct((ROWS + META, 128), BF16),
            jax.ShapeDtypeStruct((LINES, 128), F32),
            jax.ShapeDtypeStruct((routed, tokens), I32),
        ],
        scratch_shapes=[pltpu.VMEM((routed * tokens, 256), BF16)],
        compiler_params=pltpu.CompilerParams(vmem_limit_bytes=24 * 2**20),
        cost_estimate=SMALL,
        name="sort_queries",
    )(routes_t, queries_r)


def attend_kernel(kind, flags, q_ref, *refs):
    kv_count = {"own": 1, "near": 3, "far": 2}[kind]
    kv, refs = refs[:kv_count], refs[kv_count:]
    if kind == "own":
        pos_ref, out_ref, qs, os, ls, tail, starts, ps = refs
    else:
        out_ref, qs, os, ls, tail, starts = refs
    step = pl.program_id(0)
    odd, chip = flags[0], flags[1]

    def shard_parts(i, is_odd):
        if kind == "own":
            return [
                (kv[0][0, i, :256], kv[0][1, i, :256], None, False),
                (kv[0][0, i, 256:], kv[0][1, i, 256:], None, True),
            ]
        sibling = (kv[1][0, i], kv[1][1, i], None, False)
        if kind == "far" and is_odd:
            return [sibling]
        parts = [(kv[0][0, i], kv[0][1, i], None, False), sibling]
        if is_odd:
            flag = jnp.where(chip >= 1, F32(0), F32(LOW))
            parts.append((kv[2][0, i], kv[2][1, i], flag, False))
        return parts

    def work(is_odd):
        @pl.when(step == 0)
        def _():
            qs[: ROWS + META] = q_ref[...]
            os[...] = jnp.zeros_like(os)
            ls[...] = jnp.zeros_like(ls)
            firsts = qs[ROWS : ROWS + META].astype(F32)
            for g in range(GROUPS):
                starts[g] = jnp.max(firsts[g : g + 1]).astype(I32)
            if kind == "own":
                eye = iota((128, 128), 0) == iota((128, 128), 1)
                for b in range(BLOCKS):
                    picked = jnp.where(eye, pos_ref[b : b + 1], F32(0))
                    reach = jnp.sum(picked, axis=1, keepdims=True)
                    ps[b * 128 : (b + 1) * 128] = jnp.broadcast_to(reach, (128, 128))

        units = []
        for i in range(STEP):
            start = pl.multiple_of(starts[step * STEP + i] * 16, 16)
            parts = shard_parts(i, is_odd)
            for c in range(MOST_GROUP // CHUNK):
                units.append((pl.ds(pl.multiple_of(start + c * CHUNK, 16), CHUNK), parts))
        scored = []
        for rows, parts in units:
            q = qs[rows, :]
            scores = []
            for k, _, _, causal in parts:
                s = dot_t(q, k)
                if causal:
                    reach = ps[rows, :][:, :1]
                    s = jnp.where(iota(s.shape, 1).astype(F32) <= reach, s, F32(LOW))
                scores.append(s)
            scored.append(scores)
        tops = []
        for (rows, parts), scores in zip(units, scored):
            peaks = []
            for s, (_, _, bias, _) in zip(scores, parts):
                peak = jnp.max(s, axis=1, keepdims=True)
                peaks.append(peak if bias is None else peak + bias)
            tops.append(functools.reduce(jnp.maximum, peaks))
        results = []
        for (rows, parts), scores, top in zip(units, scored, tops):
            both = None
            for s, (_, v, bias, _) in zip(scores, parts):
                base = top if bias is None else top - bias
                weight = jnp.exp2((s - base) * F32(SCALE)).astype(BF16)
                product = dot(weight, jnp.concatenate([v, jnp.ones_like(v)], axis=1))
                both = product if both is None else both + product
            results.append(both)
        for (rows, parts), both, top in zip(units, results, tops):
            total = both[:, 128:]
            os[rows, :] = (both[:, :128] / total).astype(BF16)
            ls[rows, :] = top * F32(SCALE) + jnp.log2(total)

        @pl.when(step == GROUPS // STEP - 1)
        def _():
            out_ref[:ROWS] = os[:ROWS]
            eye = iota((128, 128), 0) == iota((128, 128), 1)
            tail[...] = jnp.zeros_like(tail)
            for b in range(BLOCKS):
                square = ls[b * 128 : (b + 1) * 128]
                line = jnp.sum(jnp.where(eye, square, F32(0)), axis=0, keepdims=True)
                high = line.astype(BF16).astype(F32)
                middle = (line - high).astype(BF16).astype(F32)
                tail[b : b + 1] = high
                tail[BLOCKS + b : BLOCKS + b + 1] = middle
                tail[2 * BLOCKS + b : 2 * BLOCKS + b + 1] = line - high - middle
            out_ref[ROWS:] = tail[...].astype(BF16)

    if kind == "own":
        work(False)
    else:
        pl.when(odd == 0)(lambda: work(False))
        pl.when(odd == 1)(lambda: work(True))


def attend(kind, flags, packed, kvs, pos=None):
    kv_spec = pl.BlockSpec((2, STEP, 512, 128), lambda g: (0, g, 0, 0))

    def whole(rows):
        return pl.BlockSpec((rows, 128), lambda g: (0, 0))

    in_specs = [pl.BlockSpec(memory_space=pltpu.SMEM)]
    in_specs += [whole(ROWS + META)] + [kv_spec] * len(kvs)
    args = [flags, packed, *kvs]
    scratch = [pltpu.VMEM((SPAN, 128), BF16), pltpu.VMEM((SPAN, 128), BF16), pltpu.VMEM((SPAN, 128), F32)]
    scratch += [pltpu.VMEM((TAIL, 128), F32), pltpu.SMEM((GROUPS,), I32)]
    if kind == "own":
        in_specs.append(whole(LINES))
        args.append(pos)
        scratch.append(pltpu.VMEM((SPAN, 128), F32))
    return pl.pallas_call(
        functools.partial(attend_kernel, kind),
        grid=(GROUPS // STEP,),
        in_specs=in_specs,
        out_specs=whole(ROWS + TAIL),
        out_shape=jax.ShapeDtypeStruct((ROWS + TAIL, 128), BF16),
        scratch_shapes=scratch,
        compiler_params=pltpu.CompilerParams(
            dimension_semantics=("arbitrary",), vmem_limit_bytes=LIMIT
        ),
        cost_estimate=SMALL,
        name="attend_" + kind,
    )(*args)


def lines_of(tail):
    tail = tail.astype(F32)
    return tail[:BLOCKS] + tail[BLOCKS : 2 * BLOCKS] + tail[2 * BLOCKS : 3 * BLOCKS]


def mix(lines, b, on):
    first, second = lines[0][b : b + 1], jnp.where(on, lines[1][b : b + 1], F32(LOW))
    top = jnp.maximum(first, second)
    total = jnp.exp2(first - top) + jnp.exp2(second - top)
    eye = iota((128, 128), 0) == iota((128, 128), 1)
    share = jnp.exp2(second - top) / total
    column = jnp.sum(jnp.where(eye, share, F32(0)), axis=1, keepdims=True)
    return column, top + jnp.log2(total)


def mix_kernel(flags, own_ref, back_ref, here_ref, sum_ref, lines_ref):
    odd, chip = flags[0], flags[1]

    def run(other, on):
        lines = lines_of(own_ref[ROWS:]), lines_of(other[ROWS:])
        lines_ref[...] = jnp.zeros_like(lines_ref)
        for b in range(BLOCKS):
            rows = slice(b * 128, (b + 1) * 128)
            share, line = mix(lines, b, on)
            own = own_ref[rows].astype(F32)
            sum_ref[rows] = (own + share * (other[rows].astype(F32) - own)).astype(BF16)
            lines_ref[b : b + 1] = line

    pl.when(odd == 0)(lambda: run(back_ref, chip >= 1))
    pl.when(odd == 1)(lambda: run(here_ref, odd == 1))


def mix_early(flags, own, back, here):
    return pl.pallas_call(
        mix_kernel,
        in_specs=[pl.BlockSpec(memory_space=pltpu.SMEM)] + [pl.BlockSpec(memory_space=pltpu.VMEM)] * 3,
        out_shape=[jax.ShapeDtypeStruct((ROWS, 128), BF16), jax.ShapeDtypeStruct((LINES, 128), F32)],
        compiler_params=pltpu.CompilerParams(vmem_limit_bytes=24 * 2**20),
        cost_estimate=SMALL,
        name="mix_early",
    )(flags, own, back, here)


def finish_kernel(flags, sum_ref, lines_ref, near_ref, far_ref, slots_ref, out_ref, merged):
    odd, chip = flags[0], flags[1]

    def merge(late_ref, on):
        lines = lines_ref[:BLOCKS], lines_of(late_ref[ROWS:])
        for b in range(BLOCKS):
            rows = slice(b * 128, (b + 1) * 128)
            share, _ = mix(lines, b, on)
            early = sum_ref[rows].astype(F32)
            merged[rows] = (early + share * (late_ref[rows].astype(F32) - early)).astype(BF16)

    pl.when(odd == 1)(lambda: merge(near_ref, chip >= 1))
    pl.when(odd == 0)(lambda: merge(far_ref, chip >= 2))
    entries = out_ref.shape[0]
    for e in range(entries // 256):
        rows = slice(e * 256, (e + 1) * 256)
        place = one_hot(iota((256, ROWS), 1) == slots_ref[rows])
        out_ref[rows] = dot(place, merged[...]).astype(BF16)


def finish(flags, early, lines, near, far, slots_column):
    entries = slots_column.shape[0]
    return pl.pallas_call(
        finish_kernel,
        in_specs=[pl.BlockSpec(memory_space=pltpu.SMEM)] + [pl.BlockSpec(memory_space=pltpu.VMEM)] * 5,
        out_shape=jax.ShapeDtypeStruct((entries, 128), BF16),
        scratch_shapes=[pltpu.VMEM((ROWS, 128), BF16)],
        compiler_params=pltpu.CompilerParams(vmem_limit_bytes=24 * 2**20),
        cost_estimate=SMALL,
        name="finish",
    )(flags, early, lines, near, far, slots_column)


def moved(block, distance):
    devices = range(lax.axis_size("seq"))
    pairs = [(i, i + distance(i)) for i in devices if distance(i) is not None and i + distance(i) in devices]
    return lax.ppermute(block, "seq", pairs)


def shards(queries, keys, values, routes):
    tokens, routed, width = queries.shape
    devices = range(lax.axis_size("seq"))
    device = lax.axis_index("seq").astype(I32)
    flags = jnp.stack([device % 2, device // 2])

    def after(x, *others):
        return lax.optimization_barrier((x, *others))[0]

    kv = jnp.stack([keys.transpose(1, 0, 2), values.transpose(1, 0, 2)])
    kv_forward = moved(kv, lambda i: 2 if i % 2 else None)
    packed, pos, slots = sort_queries(after(routes.T, kv), queries.transpose(1, 0, 2).reshape(-1, width))
    column = slots.T.reshape(-1, 1)
    near_q = moved(packed, lambda i: -2)
    own = attend("own", flags, packed, [kv], pos)
    kv_sibling = moved(kv, lambda i: -1 if i % 2 else 1)
    far_q = moved(after(packed, own, column), lambda i: 0 if i % 2 else -4)
    near_q = after(near_q, own)
    near_out = attend("near", flags, near_q, [kv, kv_sibling, kv_forward])
    near_back = moved(near_out, lambda i: 2)
    far_q = after(far_q, near_out)
    far_out = attend("far", flags, far_q, [kv, kv_sibling])
    far_back = moved(far_out, lambda i: None if i % 2 else 4)
    early_sum, early_lines = mix_early(flags, own, near_back, far_out)
    out = finish(flags, early_sum, early_lines, near_back, after(far_back, early_sum), column)
    return out.reshape(tokens, routed, width)


def solution(mesh):
    placed = (P("seq", None, None), P("seq", None, None), P("seq", None, None), P("seq", None))
    return jax.shard_map(
        shards, mesh=mesh, in_specs=placed, out_specs=P("seq", None, None), check_vma=False
    )
```
